32 devices in a mesh: groups: 2 (over y), slab: 4 (over z), angle: 4 (over x, core).
Axes of the slice: x: 2, y: 2, z: 4, core: 2. Of those that a mesh axis runs over, the one named last changes fastest.
Arguments:
- activity: bfloat16 [12288, 128], P(('groups', 'slab')), parts along dimension 0, may hold values from 0.19921875 to 5
- sensitivity: float32 [12288], P(('groups', 'slab')), parts along dimension 0, may hold values from 8 to 64
- system_tiles: bfloat16 [8, 4, 86, 128, 128], P(('groups', 'slab'), 'angle'), parts along dimension 0, may hold values from 1.5616417e-05 to 0.0078125
- tile_voxel: int32 [8, 4, 86], P(('groups', 'slab'), 'angle'), parts along dimension 0, may hold values from 0 to 11, as said below
- tile_line: int32 [8, 4, 86], P(('groups', 'slab'), 'angle'), parts along dimension 0, may hold values from 0 to 8, as said below
- oblique_rows: int32 [8, 4, 2], P(('groups', 'slab'), 'angle'), parts along dimension 0, may hold values from 0 to 3, as said below
- counts: int32 [8, 4, 512, 128], P(('groups', 'slab'), 'angle'), parts along dimension 0, may hold values from 0 to 11
- background: bfloat16 [8, 4, 512, 128], P(('groups', 'slab'), 'angle'), parts along dimension 0, may hold values from 0.5 to 4
Outputs:
- updated: bfloat16 [12288, 128], P(('groups', 'slab')), parts along dimension 0
The draws below stay inside these ranges and needn't reach their ends.
There are 2 independent parts, one for each index of `groups`. The reference program is written for one: setup_inputs(seed, part) draws one part's arguments, and reference() takes and returns one part's arrays. A program takes and returns all parts, laid end to end along the dimension named above; each array names one. Nothing has to cross between parts.
Inputs may be any that keep to these rules, and one draw needn't show every extreme that they name: On each slab and angle the used slots come first; an unused slot has tile_line 8 and tile_voxel 0. Used slots of one slab and angle name distinct pairs of voxel block and local LOR block, sorted by voxel block then LOR block. Every draw has a slab and angle with all 86 slots used. `tile_line`: see tile_voxel; the value 8 marks an unused slot. `oblique_rows`: the 2 entries of one slab and angle are distinct.
All inputs are finite; a program needn't handle non-finite values.
Results may differ from the reference program's by a relative error of at most 0.0022.
Values may be sent and summed in bfloat16 or wider, within the bound.
No kernel may reach another device: no remote copies, remote signals or barrier semaphores. Data moves between devices by JAX's collectives and lax.ppermute only.
A program may use at most 64 MiB of HBM per device.

```python
import math
import jax
import jax.numpy as jnp
from jax import lax

BLK = 128
FRAMES = 128
VB_DEV = 12
LOR_OWN = 4
LOR_OBL = 2
TILES = 86
VOXELS = 6144
N_SLAB = 4
N_ANGLE = 4


def tile_lists(key):
    devices = N_SLAB * N_ANGLE
    local_blocks = LOR_OWN + 2 * LOR_OBL
    pairs = VB_DEV * local_blocks
    device_keys = jax.random.split(jax.random.fold_in(key, 11), devices)
    orders = jax.vmap(lambda device_key: jax.random.permutation(device_key, pairs))(device_keys)[:, :TILES]
    orders = orders.astype(jnp.int32)
    numbers = jnp.arange(devices, dtype=jnp.int32)
    slab_number = numbers // N_ANGLE
    angle_number = numbers % N_ANGLE
    edgeness = jnp.abs(2 * slab_number + 1 - N_SLAB)
    jitter = jax.random.randint(jax.random.fold_in(key, 12), (devices,), 0, TILES // 8 + 1, dtype=jnp.int32)
    dropped = TILES // 2 * edgeness // N_SLAB + jitter
    filled = (slab_number == N_SLAB // 2) & (angle_number == 0)
    dropped = jnp.where(filled, 0, dropped)
    live_count = TILES - dropped
    position = jnp.arange(TILES, dtype=jnp.int32)[None, :]
    in_use = position < live_count[:, None]
    keyed = jnp.where(in_use, orders, pairs)
    keyed = jnp.sort(keyed, axis=1)
    in_use = keyed < pairs
    voxel = jnp.where(in_use, keyed // local_blocks, 0).astype(jnp.int32)
    line_block = jnp.where(in_use, keyed % local_blocks, local_blocks).astype(jnp.int32)
    return (voxel.reshape(N_SLAB, N_ANGLE, TILES), line_block.reshape(N_SLAB, N_ANGLE, TILES))


def draw_tile_voxel(key, part):
    return tile_lists(key)[0]


def draw_tile_line(key, part):
    return tile_lists(key)[1]


def draw_oblique_rows(key, part):
    key = jax.random.fold_in(key, 5)
    devices = N_SLAB * N_ANGLE
    device_keys = jax.random.split(key, devices)
    chosen = jax.vmap(lambda device_key: jax.random.permutation(device_key, LOR_OWN))(device_keys)[:, :LOR_OBL]
    return chosen.astype(jnp.int32).reshape(N_SLAB, N_ANGLE, LOR_OBL)


def touch_ends(drawn, rng, smallest, top_value):
    place = [jax.random.randint(jax.random.fold_in(rng, axis), (), 0, length) for axis, length in enumerate(drawn.shape)]
    widest = drawn.shape.index(max(drawn.shape))
    neighbour = place[:widest] + [(place[widest] + 1) % drawn.shape[widest]] + place[widest + 1:]
    return drawn.at[tuple(place)].set(smallest).at[tuple(neighbour)].set(top_value)


def steps_of(rng, shape, cuts, least, top_value):
    def one(axis_at, parts):
        draws = jax.random.uniform(jax.random.fold_in(jax.random.fold_in(rng, 6), axis_at), (parts,), jnp.float32, least / len(cuts), top_value / len(cuts))
        return jnp.repeat(jnp.exp(draws), shape[axis_at] // parts).reshape((-1,) + (1,) * (len(shape) - axis_at - 1))

    gain = one(*cuts[0])
    for cut in cuts[1:]:
        gain = gain * one(*cut)
    return gain


def setup_inputs(seed: int = 0, part: int = 0) -> dict:
    keys = jax.random.split(jax.random.key(seed), 9)
    part_splits = jax.random.split(jax.random.fold_in(keys[8], part), 9)
    activity = jnp.clip(jnp.exp(math.log(5.0) - 3.2227897 * jax.random.uniform(part_splits[0], (VOXELS, FRAMES), jnp.float32) ** steps_of(part_splits[0], (VOXELS, FRAMES), ((0, 4),), -0.2, 0.2)), 0.19921875, 5.0).astype(jnp.bfloat16)
    sensitivity = jnp.clip(jnp.exp(math.log(64.0) - 2.0794415 * jax.random.uniform(part_splits[1], (VOXELS,), jnp.float32) ** steps_of(part_splits[1], (VOXELS,), ((0, 4),), -0.2, 0.2)), 8.0, 64.0)
    system_tiles = jnp.clip(jnp.exp(math.log(0.0078125) - 6.2151576 * jax.random.uniform(part_splits[2], (N_SLAB, N_ANGLE, TILES, BLK, BLK), jnp.float32) ** steps_of(part_splits[2], (N_SLAB, N_ANGLE, TILES, BLK, BLK), ((0, 4), (1, 4)), -0.2, 0.2)), 1.5616416931152344e-05, 0.0078125).astype(jnp.bfloat16)
    tile_voxel = draw_tile_voxel(jax.random.fold_in(jax.random.fold_in(keys[8], part), 71), part)
    tile_line = draw_tile_line(jax.random.fold_in(jax.random.fold_in(keys[8], part), 71), part)
    oblique_rows = draw_oblique_rows(jax.random.fold_in(jax.random.fold_in(keys[8], part), 71), part)
    counts = touch_ends(jax.random.randint(part_splits[6], (N_SLAB, N_ANGLE, LOR_OWN * BLK, FRAMES), 0, 12), jax.random.fold_in(part_splits[6], 1), 0, 11).astype(jnp.int32)
    background = jnp.clip(jnp.exp(math.log(4.0) - 2.0794415 * jax.random.uniform(part_splits[7], (N_SLAB, N_ANGLE, LOR_OWN * BLK, FRAMES), jnp.float32) ** steps_of(part_splits[7], (N_SLAB, N_ANGLE, LOR_OWN * BLK, FRAMES), ((0, 4), (1, 4)), -0.2, 0.2)), 0.5, 4.0).astype(jnp.bfloat16)
    return dict(activity=activity, sensitivity=sensitivity, system_tiles=system_tiles, tile_voxel=tile_voxel, tile_line=tile_line, oblique_rows=oblique_rows, counts=counts, background=background)


def forward_slab(inputs):
    slab_blocks, slab_tiles, voxel_index, line_index = inputs
    highest = lax.Precision.HIGHEST
    local_blocks = LOR_OWN + 2 * LOR_OBL
    gathered = jnp.take(slab_blocks, voxel_index, axis=0).astype(jnp.float32)
    per_tile = jnp.einsum("kvl,kvf->klf", slab_tiles.astype(jnp.float32), gathered, precision=highest)
    onehot = (line_index[:, None] == jnp.arange(local_blocks, dtype=jnp.int32)[None, :]).astype(jnp.float32)
    return jnp.einsum("kj,klf->jlf", onehot, per_tile, precision=highest)


def backward_slab(inputs):
    slab_tiles, voxel_index, line_index, local_ratio = inputs
    highest = lax.Precision.HIGHEST
    local_blocks = LOR_OWN + 2 * LOR_OBL
    clamped = jnp.minimum(line_index, local_blocks - 1)
    picked = jnp.take(local_ratio, clamped, axis=0).astype(jnp.float32)
    picked = jnp.where((line_index < local_blocks)[:, None, None], picked, jnp.float32(0.0))
    per_voxel = jnp.einsum("kvl,klf->kvf", slab_tiles.astype(jnp.float32), picked, precision=highest)
    onehot = (voxel_index[:, None] == jnp.arange(VB_DEV, dtype=jnp.int32)[None, :]).astype(jnp.float32)
    return jnp.einsum("kb,kvf->bvf", onehot, per_voxel, precision=highest)


def take_rows(values, indices):
    return jnp.take(values, indices, axis=0)


def reference(activity, sensitivity, system_tiles, tile_voxel, tile_line, oblique_rows, counts, background):
    highest = lax.Precision.HIGHEST
    blocks = activity.reshape(N_SLAB, VB_DEV, BLK, FRAMES)

    def angle_step(accumulated, angle_now):
        slab_tiles = lax.dynamic_index_in_dim(system_tiles, angle_now, 1, keepdims=False)
        voxel_index = lax.dynamic_index_in_dim(tile_voxel, angle_now, 1, keepdims=False)
        line_index = lax.dynamic_index_in_dim(tile_line, angle_now, 1, keepdims=False)
        oblique_table = lax.dynamic_index_in_dim(oblique_rows, angle_now, 1, keepdims=False)
        measured = lax.dynamic_index_in_dim(counts, angle_now, 1, keepdims=False)
        additive = lax.dynamic_index_in_dim(background, angle_now, 1, keepdims=False)
        partial_value = lax.map(forward_slab, (blocks, slab_tiles, voxel_index, line_index))
        own_part = partial_value[:, :LOR_OWN]
        left_slots = partial_value[:, LOR_OWN:LOR_OWN + LOR_OBL]
        right_slots = partial_value[:, LOR_OWN + LOR_OBL:]
        nothing = jnp.zeros_like(left_slots[:1])
        from_left = jnp.concatenate([nothing, right_slots[:-1]], axis=0)
        from_right = jnp.concatenate([left_slots[1:], nothing], axis=0)
        oblique_select = (oblique_table[:, :, None] == jnp.arange(LOR_OWN, dtype=jnp.int32)[None, None, :]).astype(jnp.float32)
        projection = own_part + jnp.einsum("sjo,sjlf->solf", oblique_select, from_left + from_right, precision=highest)
        measured = measured.reshape(N_SLAB, LOR_OWN, BLK, FRAMES).astype(jnp.float32)
        additive = additive.reshape(N_SLAB, LOR_OWN, BLK, FRAMES).astype(jnp.float32)
        ratios = (measured / (projection + additive)).astype(jnp.bfloat16)
        oblique_ratio = jax.vmap(take_rows)(ratios, oblique_table)
        empty_ratio = jnp.zeros_like(oblique_ratio[:1])
        from_before = jnp.concatenate([empty_ratio, oblique_ratio[:-1]], axis=0)
        from_after = jnp.concatenate([oblique_ratio[1:], empty_ratio], axis=0)
        local_ratio = jnp.concatenate([ratios, from_before, from_after], axis=1)
        backward = lax.map(backward_slab, (slab_tiles, voxel_index, line_index, local_ratio))
        return accumulated + backward, None

    start_sum = jnp.zeros((N_SLAB, VB_DEV, BLK, FRAMES), jnp.float32)
    accumulated = lax.scan(angle_step, start_sum, jnp.arange(N_ANGLE, dtype=jnp.int32))[0]
    backprojection = accumulated.reshape(N_SLAB * VB_DEV * BLK, FRAMES)
    return (activity.astype(jnp.float32) * backprojection / sensitivity[:, None]).astype(jnp.bfloat16)
```

```python
import functools

import jax
import jax.numpy as jnp
from jax import lax
from jax.experimental import pallas as pl
from jax.experimental.pallas import tpu as pltpu
from jax.sharding import PartitionSpec as P

VMEM = pl.BlockSpec(memory_space=pltpu.VMEM)
SMEM = pl.BlockSpec(memory_space=pltpu.SMEM)
PART_SCALE = 256.0
CHIP_SCALE = 128.0


def params(**more):
    return pltpu.CompilerParams(vmem_limit_bytes=16 * 1024 * 1024, **more)


def index_tiles(voxel_ref, line_ref, slot_ref, blocks, lines):
    stride = lines + 1
    for n in range(blocks * stride):
        slot_ref[n] = -1
    for k in range(voxel_ref.shape[-1]):
        slot_ref[voxel_ref[k] * stride + line_ref[k]] = k


def tile_of(tiles_ref, slot_ref, voxel, line, lines):
    slot = slot_ref[voxel * (lines + 1) + line]
    tile = tiles_ref[jnp.maximum(slot, 0)]
    return jnp.where(slot >= 0, tile, jnp.zeros_like(tile))


def project(image_ref, tiles_ref, slot_ref, first, count, blocks, lines):
    weights = jnp.concatenate(
        [
            jnp.concatenate(
                [tile_of(tiles_ref, slot_ref, v, first + c, lines) for c in range(count)], axis=1
            )
            for v in range(blocks)
        ],
        axis=0,
    )
    return jnp.dot(image_ref[...], weights, preferred_element_type=jnp.float32)


def edge_kernel(
    blocks, own, lines, place_ref, voxel_ref, line_ref, activity_ref, tiles_ref,
    forth_ref, back_ref, image_ref, slot_ref,
):
    size = tiles_ref.shape[-1]
    width = (lines - own) // 2
    index_tiles(voxel_ref, line_ref, slot_ref, blocks, lines)
    for v in range(blocks):
        image_ref[:, v * size : (v + 1) * size] = activity_ref[v * size : (v + 1) * size, :].T
    odd = place_ref[0]
    for out_ref, first in (
        (forth_ref, own + width * (1 - odd)),
        (back_ref, own + width * odd),
    ):
        sums = project(image_ref, tiles_ref, slot_ref, first, width, blocks, lines)
        for c in range(width):
            out_ref[c] = sums[:, c * size : (c + 1) * size].astype(out_ref.dtype)


def own_kernel(
    blocks, own, lines, voxel_ref, line_ref, image_ref, tiles_ref, counts_ref, background_ref,
    base_ref, ratio_ref, slot_ref,
):
    size = tiles_ref.shape[-1]
    index_tiles(voxel_ref, line_ref, slot_ref, blocks, lines)
    for first in range(0, own, 2):
        sums = project(image_ref, tiles_ref, slot_ref, first, 2, blocks, lines)
        for c in range(2):
            o = first + c
            base = sums[:, c * size : (c + 1) * size].T + background_ref[o].astype(jnp.float32)
            base_ref[o] = base
            ratio_ref[o] = (counts_ref[o].astype(jnp.float32) / base).astype(ratio_ref.dtype)


def oblique_kernel(
    place_ref, rows_ref, forth_ref, back_ref, base_ref, counts_ref, out_ref,
):
    has_forth = place_ref[1] > 0
    has_back = place_ref[2] > 0
    for j in range(out_ref.shape[0]):
        row = rows_ref[j]
        forth = forth_ref[j].astype(jnp.float32)
        back = back_ref[j].astype(jnp.float32)
        extra = jnp.where(has_forth, forth, 0.0) + jnp.where(has_back, back, 0.0)
        total = base_ref[row] + extra.T
        out_ref[j] = (counts_ref[row].astype(jnp.float32) / total).astype(out_ref.dtype)


def back_project(ratios, tiles_ref, slot_ref, voxels, firsts, lines):
    rows = jnp.concatenate(
        [
            jnp.concatenate(
                [tile_of(tiles_ref, slot_ref, v, c, lines) for c in firsts], axis=1
            )
            for v in voxels
        ],
        axis=0,
    )
    return jnp.dot(rows, ratios, preferred_element_type=jnp.float32)


def own_back_kernel(
    blocks, own, lines, rows_ref, voxel_ref, line_ref, tiles_ref, ratio_ref, oblique_ref,
    out_ref, slot_ref, mixed_ref,
):
    size = tiles_ref.shape[-1]
    index_tiles(voxel_ref, line_ref, slot_ref, blocks, lines)
    mixed_ref[...] = ratio_ref[...]
    for j in range(oblique_ref.shape[0]):
        mixed_ref[rows_ref[j]] = oblique_ref[j]
    ratios = mixed_ref[...].reshape(own * size, -1)
    out_ref[...] = back_project(
        ratios, tiles_ref, slot_ref, range(blocks), range(own), lines
    ).reshape(out_ref.shape)


def edge_back_kernel(
    blocks, own, lines, other, scale, place_ref, voxel_ref, line_ref, tiles_ref, forth_ref,
    back_ref, own_ref, out_ref, slot_ref,
):
    size = tiles_ref.shape[-1]
    width = (lines - own) // 2
    half = blocks // 2
    index_tiles(voxel_ref, line_ref, slot_ref, blocks, lines)
    odd = place_ref[0]
    forth = jnp.where(place_ref[1] > 0, forth_ref[...], jnp.zeros_like(forth_ref))
    back = jnp.where(place_ref[2] > 0, back_ref[...], jnp.zeros_like(back_ref))
    ratios = jnp.concatenate([forth, back], axis=0).reshape(2 * width * size, -1)
    firsts = [own + width * odd + c for c in range(width)]
    firsts += [own + width * (1 - odd) + c for c in range(width)]
    start = (1 - odd if other else odd) * half
    sums = back_project(
        ratios, tiles_ref, slot_ref, [start + n for n in range(half)], firsts, lines
    ).reshape(half, size, -1)
    total = (sums + own_ref[pl.ds(start, half)]) * scale
    out_ref[...] = total.astype(out_ref.dtype)


def body(
    slabs, angles, activity, sensitivity, system_tiles, tile_voxel, tile_line, oblique_rows,
    counts, background,
):
    size = system_tiles.shape[-1]
    frames = activity.shape[1]
    blocks = activity.shape[0] // size
    own = counts.shape[2] // size
    width = oblique_rows.shape[-1]
    lines = own + 2 * width
    half = blocks // 2
    tiles = system_tiles[0, 0]
    voxel = tile_voxel[0, 0]
    line = tile_line[0, 0]
    rows = oblique_rows[0, 0]
    measured = counts[0, 0].reshape(own, size, frames)
    additive = background[0, 0].reshape(own, size, frames)

    slab = lax.axis_index("slab")
    odd = lax.axis_index("angle") % 2
    left = slab > 0
    right = slab < slabs - 1
    place = jnp.stack(
        [
            odd,
            jnp.where(odd == 0, left, right).astype(jnp.int32),
            jnp.where(odd == 0, right, left).astype(jnp.int32),
        ]
    ).astype(jnp.int32)

    forth = []
    for s in range(slabs):
        for a in range(angles):
            t = s + 1 if a % 2 == 0 else s - 1
            here = s * angles + a
            there = t * angles + a if 0 <= t < slabs else s * angles + (a ^ 1)
            forth.append((here, there))
    back = [(there, here) for here, there in forth]
    both = ("slab", "angle")
    slots = pltpu.SMEM((blocks * (lines + 1),), jnp.int32)

    def block_out(count, dtype, first=size, second=frames):
        return jax.ShapeDtypeStruct((count, first, second), dtype)

    edge_forth, edge_back, image = pl.pallas_call(
        functools.partial(edge_kernel, blocks, own, lines),
        out_shape=(
            block_out(width, jnp.bfloat16, frames, size),
            block_out(width, jnp.bfloat16, frames, size),
            jax.ShapeDtypeStruct((frames, blocks * size), jnp.bfloat16),
        ),
        in_specs=[SMEM, SMEM, SMEM, VMEM, VMEM],
        out_specs=(VMEM, VMEM, VMEM),
        scratch_shapes=[slots],
        compiler_params=params(),
        name="edge_partials",
    )(place, voxel, line, activity, tiles)
    got_forth = lax.ppermute(edge_forth, both, forth)
    got_back = lax.ppermute(edge_back, both, back)
    base, ratio = pl.pallas_call(
        functools.partial(own_kernel, blocks, own, lines),
        out_shape=(block_out(own, jnp.float32), block_out(own, jnp.bfloat16)),
        in_specs=[SMEM, SMEM, VMEM, VMEM, VMEM, VMEM],
        out_specs=(VMEM, VMEM),
        scratch_shapes=[slots],
        compiler_params=params(),
        name="own_partials",
    )(voxel, line, image, tiles, measured, additive)
    oblique = pl.pallas_call(
        oblique_kernel,
        out_shape=block_out(width, jnp.bfloat16),
        in_specs=[SMEM, SMEM, VMEM, VMEM, VMEM, VMEM],
        out_specs=VMEM,
        compiler_params=params(),
        name="oblique_ratios",
    )(place, rows, got_forth, got_back, base, measured)
    beside_forth = lax.ppermute(oblique, both, forth)
    beside_back = lax.ppermute(oblique, both, back)
    own_back = pl.pallas_call(
        functools.partial(own_back_kernel, blocks, own, lines),
        out_shape=block_out(blocks, jnp.float32),
        in_specs=[SMEM, SMEM, SMEM, VMEM, VMEM, VMEM],
        out_specs=VMEM,
        scratch_shapes=[slots, pltpu.VMEM((own, size, frames), jnp.bfloat16)],
        compiler_params=params(),
        name="own_back",
    )(rows, voxel, line, tiles, ratio, oblique)

    def edge_half(other, scale, dtype, name):
        return pl.pallas_call(
            functools.partial(edge_back_kernel, blocks, own, lines, other, scale),
            out_shape=block_out(half, dtype),
            in_specs=[SMEM, SMEM, SMEM, VMEM, VMEM, VMEM, VMEM],
            out_specs=VMEM,
            scratch_shapes=[slots],
            compiler_params=params(),
            name=name,
        )(place, voxel, line, tiles, beside_forth, beside_back, own_back)

    half_rows = half * size
    mine = odd * half_rows
    image_rows = lax.dynamic_slice_in_dim(activity, mine, half_rows, 0).astype(jnp.float32)
    sens_rows = lax.dynamic_slice_in_dim(sensitivity, mine, half_rows, 0)
    pairs = [(a, a ^ 1) for a in range(angles)]
    sent = edge_half(True, PART_SCALE, jnp.float32, "edge_back_sent").astype(jnp.float16)
    got = lax.ppermute(sent, "angle", pairs)
    kept = edge_half(False, 1.0, jnp.float32, "edge_back_kept")
    chip = kept + got.astype(jnp.float32) * (1.0 / PART_SCALE)
    if angles == 4:
        chip = (chip * CHIP_SCALE).astype(jnp.float16)
        beside = lax.ppermute(chip, "angle", [(a, a ^ 2) for a in range(angles)])
        total = (chip.astype(jnp.float32) + beside.astype(jnp.float32)) * (1.0 / CHIP_SCALE)
    else:
        groups = [list(range(odd_one, angles, 2)) for odd_one in range(2)]
        total = lax.psum(chip, "angle", axis_index_groups=groups)
    total = total.reshape(half_rows, frames)
    new_rows = (image_rows * total / sens_rows[:, None]).astype(jnp.bfloat16)
    other_rows = lax.ppermute(new_rows, "angle", pairs)
    low = jnp.where(odd == 0, new_rows, other_rows)
    high = jnp.where(odd == 0, other_rows, new_rows)
    return jnp.concatenate([low, high], axis=0)


def solution(mesh):
    placed = (
        P(("groups", "slab"), None),
        P(("groups", "slab")),
        P(("groups", "slab"), "angle", None, None, None),
        P(("groups", "slab"), "angle", None),
        P(("groups", "slab"), "angle", None),
        P(("groups", "slab"), "angle", None),
        P(("groups", "slab"), "angle", None, None),
        P(("groups", "slab"), "angle", None, None),
    )
    return jax.shard_map(
        functools.partial(body, mesh.shape["slab"], mesh.shape["angle"]),
        mesh=mesh,
        in_specs=placed,
        out_specs=P(("groups", "slab"), None),
        check_vma=False,
    )
```

```python
import functools

import jax
import jax.numpy as jnp
from jax import lax
from jax.experimental import pallas as pl
from jax.experimental.pallas import tpu as pltpu
from jax.sharding import PartitionSpec as P

VMEM = pl.BlockSpec(memory_space=pltpu.VMEM)
SMEM = pl.BlockSpec(memory_space=pltpu.SMEM)
HBM = pl.BlockSpec(memory_space=pltpu.HBM)
PART_SCALE = 256.0
CHIP_SCALE = 128.0
GROUP = 4
PIECE = 8


def params(mebibytes=16):
    return pltpu.CompilerParams(vmem_limit_bytes=mebibytes * 1024 * 1024)


def place(slabs):
    slab = lax.axis_index("slab")
    odd = lax.axis_index("angle") % 2
    left = slab > 0
    right = slab < slabs - 1
    even = odd == 0
    forth = jnp.logical_or(jnp.logical_and(even, left), jnp.logical_and(~even, right))
    back = jnp.logical_or(jnp.logical_and(even, right), jnp.logical_and(~even, left))
    return odd, forth, back


def index_tiles(voxel_ref, line_ref, slot_ref, blocks, lines):
    stride = lines + 1
    for n in range(blocks * stride):
        slot_ref[n] = -1
    for k in range(voxel_ref.shape[-1]):
        slot_ref[voxel_ref[k] * stride + line_ref[k]] = k


def tile_of(tiles_ref, slot_ref, voxel, line, lines):
    slot = slot_ref[voxel * (lines + 1) + line]
    tile = tiles_ref[jnp.maximum(slot, 0)]
    return jnp.where(slot >= 0, tile, jnp.zeros_like(tile))


def project(image, tiles_ref, slot_ref, voxels, which, lines):
    weights = jnp.concatenate(
        [
            jnp.concatenate([tile_of(tiles_ref, slot_ref, v, c, lines) for c in which], axis=1)
            for v in voxels
        ],
        axis=0,
    )
    return jnp.dot(image, weights, preferred_element_type=jnp.float32)


def edge_kernel(
    blocks, own, lines, voxel_hbm, line_hbm, activity_hbm, tiles_hbm,
    forth_ref, back_ref, image_ref, tiles_ref,
    voxel_ref, line_ref, activity_ref, slot_ref, small_sem, tile_sem,
):
    size = tiles_ref.shape[-1]
    total = tiles_ref.shape[0]
    width = (lines - own) // 2
    first = [
        pltpu.make_async_copy(voxel_hbm, voxel_ref, small_sem.at[0]),
        pltpu.make_async_copy(line_hbm, line_ref, small_sem.at[1]),
        pltpu.make_async_copy(activity_hbm, activity_ref, small_sem.at[2]),
    ]
    pieces = []
    for n, start in enumerate(range(0, total, PIECE)):
        span = pl.ds(start, min(PIECE, total - start))
        pieces.append(
            pltpu.make_async_copy(tiles_hbm.at[span], tiles_ref.at[span], tile_sem.at[n])
        )
    for copy in first + pieces:
        copy.start()
    first[0].wait()
    first[1].wait()
    index_tiles(voxel_ref, line_ref, slot_ref, blocks, lines)
    first[2].wait()
    for v in range(blocks):
        image_ref[:, v * size : (v + 1) * size] = activity_ref[v * size : (v + 1) * size, :].T
    odd = lax.axis_index("angle") % 2
    outs = (
        (forth_ref, own + width * (1 - odd)),
        (back_ref, own + width * odd),
    )
    sums = [None, None]
    waited = 0
    for low in range(0, blocks, GROUP):
        high = min(low + GROUP, blocks)
        needed = len(pieces) if high == blocks else min(len(pieces), pl.cdiv(high * lines, PIECE))
        for copy in pieces[waited:needed]:
            copy.wait()
        waited = needed
        image = image_ref[:, low * size : high * size]
        for n, (_, start) in enumerate(outs):
            which = [start + c for c in range(width)]
            part = project(image, tiles_ref, slot_ref, range(low, high), which, lines)
            sums[n] = part if sums[n] is None else sums[n] + part
    for n, (out_ref, _) in enumerate(outs):
        for c in range(width):
            out_ref[c] = sums[n][:, c * size : (c + 1) * size].astype(out_ref.dtype)


def own_kernel(
    blocks, own, lines, voxel_ref, line_ref, rows_ref, image_ref, tiles_ref, counts_ref,
    background_ref, base_ref, measured_ref, ratio_ref, matrix_ref, slot_ref, order_ref,
):
    size = tiles_ref.shape[-1]
    width = (lines - own) // 2
    half = blocks // 2
    index_tiles(voxel_ref, line_ref, slot_ref, blocks, lines)
    for j in range(width):
        order_ref[j] = rows_ref[j]
    at = jnp.int32(width)
    for o in range(own):
        oblique = functools.reduce(jnp.logical_or, [rows_ref[j] == o for j in range(width)])
        order_ref[jnp.where(oblique, own, at)] = o
        at = at + jnp.where(oblique, 0, 1)
    image = image_ref[...]
    for start in range(0, own, width):
        which = [order_ref[start + c] for c in range(width)]
        sums = project(image, tiles_ref, slot_ref, range(blocks), which, lines)
        for c, row in enumerate(which):
            base = sums[:, c * size : (c + 1) * size].T + background_ref[row].astype(jnp.float32)
            measured = counts_ref[row].astype(jnp.float32)
            if start == 0:
                base_ref[c] = base
                measured_ref[c] = measured
            else:
                ratio_ref[start - width + c] = (measured / base).astype(ratio_ref.dtype)
    away = (1 - lax.axis_index("angle") % 2) * half
    for v in range(blocks):
        voxel = away + v if v < half else half - away + v - half
        for c in range(lines):
            line = order_ref[c] if c < own else c
            matrix_ref[v * size : (v + 1) * size, c * size : (c + 1) * size] = tile_of(
                tiles_ref, slot_ref, voxel, line, lines
            )


def oblique_kernel(slabs, forth_ref, back_ref, base_ref, measured_ref, out_ref):
    _, has_forth, has_back = place(slabs)
    for j in range(out_ref.shape[0]):
        forth = forth_ref[j].astype(jnp.float32)
        back = back_ref[j].astype(jnp.float32)
        extra = jnp.where(has_forth, forth, 0.0) + jnp.where(has_back, back, 0.0)
        out_ref[j] = (measured_ref[j] / (base_ref[j] + extra.T)).astype(out_ref.dtype)


def own_back_kernel(own, matrix_ref, oblique_ref, ratio_ref, out_ref):
    size = ratio_ref.shape[1]
    ratios = jnp.concatenate([oblique_ref[...], ratio_ref[...]], axis=0)
    ratios = ratios.reshape(own * size, -1)
    out_ref[...] = jnp.dot(
        matrix_ref[:, : own * size], ratios, preferred_element_type=jnp.float32
    )


def edge_back_kernel(slabs, own, start, scale, matrix_ref, forth_ref, back_ref, own_ref, out_ref):
    size = forth_ref.shape[1]
    rows = out_ref.shape[0]
    odd, has_forth, has_back = place(slabs)
    forth = jnp.where(has_forth, forth_ref[...], jnp.zeros_like(forth_ref))
    back = jnp.where(has_back, back_ref[...], jnp.zeros_like(back_ref))
    left = jnp.where(odd == 0, forth, back)
    right = jnp.where(odd == 0, back, forth)
    ratios = jnp.concatenate([left, right], axis=0)
    ratios = ratios.reshape(ratios.shape[0] * size, -1)
    sums = jnp.dot(
        matrix_ref[start : start + rows, own * size :], ratios, preferred_element_type=jnp.float32
    )
    out_ref[...] = (sums + own_ref[start : start + rows]) * scale


def body(
    slabs, angles, activity, sensitivity, system_tiles, tile_voxel, tile_line, oblique_rows,
    counts, background,
):
    size = system_tiles.shape[-1]
    frames = activity.shape[1]
    blocks = activity.shape[0] // size
    own = counts.shape[2] // size
    width = oblique_rows.shape[-1]
    lines = own + 2 * width
    half = blocks // 2
    tiles = system_tiles[0, 0]
    voxel = tile_voxel[0, 0]
    line = tile_line[0, 0]
    rows = oblique_rows[0, 0]
    measured = counts[0, 0].reshape(own, size, frames)
    additive = background[0, 0].reshape(own, size, frames)

    forth = []
    for s in range(slabs):
        for a in range(angles):
            t = s + 1 if a % 2 == 0 else s - 1
            here = s * angles + a
            there = t * angles + a if 0 <= t < slabs else s * angles + (a ^ 1)
            forth.append((here, there))
    back = [(there, here) for here, there in forth]
    both = ("slab", "angle")
    slots = pltpu.SMEM((blocks * (lines + 1),), jnp.int32)

    def array(dtype, *shape):
        return jax.ShapeDtypeStruct(shape, dtype)

    edge_forth, edge_back, image, held = pl.pallas_call(
        functools.partial(edge_kernel, blocks, own, lines),
        out_shape=(
            array(jnp.bfloat16, width, frames, size),
            array(jnp.bfloat16, width, frames, size),
            array(jnp.bfloat16, frames, blocks * size),
            array(jnp.bfloat16, *tiles.shape),
        ),
        in_specs=[HBM] * 4,
        out_specs=(VMEM,) * 4,
        scratch_shapes=[
            pltpu.SMEM(voxel.shape, jnp.int32),
            pltpu.SMEM(line.shape, jnp.int32),
            pltpu.VMEM(activity.shape, activity.dtype),
            slots,
            pltpu.SemaphoreType.DMA((3,)),
            pltpu.SemaphoreType.DMA((pl.cdiv(tiles.shape[0], PIECE),)),
        ],
        compiler_params=params(),
        name="edge_partials",
    )(*[pltpu.with_memory_space_constraint(a, pltpu.HBM) for a in (voxel, line, activity, tiles)])
    got_forth = lax.ppermute(edge_forth, both, forth)
    got_back = lax.ppermute(edge_back, both, back)
    base, taken, ratio, matrix = pl.pallas_call(
        functools.partial(own_kernel, blocks, own, lines),
        out_shape=(
            array(jnp.float32, width, size, frames),
            array(jnp.float32, width, size, frames),
            array(jnp.bfloat16, own - width, size, frames),
            array(jnp.bfloat16, blocks * size, lines * size),
        ),
        in_specs=[SMEM] * 3 + [VMEM] * 4,
        out_specs=(VMEM,) * 4,
        scratch_shapes=[slots, pltpu.SMEM((own + 1,), jnp.int32)],
        compiler_params=params(),
        name="own_partials",
    )(voxel, line, rows, image, held, measured, additive)
    oblique = pl.pallas_call(
        functools.partial(oblique_kernel, slabs),
        out_shape=array(jnp.bfloat16, width, size, frames),
        in_specs=[VMEM] * 4,
        out_specs=VMEM,
        compiler_params=params(),
        name="oblique_ratios",
    )(got_forth, got_back, base, taken)
    beside_forth = lax.ppermute(oblique, both, forth)
    beside_back = lax.ppermute(oblique, both, back)
    own_back = pl.pallas_call(
        functools.partial(own_back_kernel, own),
        out_shape=array(jnp.float32, blocks * size, frames),
        in_specs=[VMEM] * 3,
        out_specs=VMEM,
        compiler_params=params(),
        name="own_back",
    )(matrix, oblique, ratio)

    half_rows = half * size

    def edge_half(start, scale, name):
        return pl.pallas_call(
            functools.partial(edge_back_kernel, slabs, own, start, scale),
            out_shape=array(jnp.float32, half_rows, frames),
            in_specs=[VMEM] * 4,
            out_specs=VMEM,
            compiler_params=params(),
            name=name,
        )(matrix, beside_forth, beside_back, own_back)

    odd = lax.axis_index("angle") % 2
    mine = odd * half_rows
    image_rows = lax.dynamic_slice_in_dim(activity, mine, half_rows, 0).astype(jnp.float32)
    sens_rows = lax.dynamic_slice_in_dim(sensitivity, mine, half_rows, 0)
    pairs = [(a, a ^ 1) for a in range(angles)]
    sent = edge_half(0, PART_SCALE, "edge_back_sent").astype(jnp.float16)
    got = lax.ppermute(sent, "angle", pairs)
    kept = edge_half(half_rows, 1.0, "edge_back_kept")
    chip = kept + got.astype(jnp.float32) * (1.0 / PART_SCALE)
    if angles == 4:
        chip = (chip * CHIP_SCALE).astype(jnp.float16)
        beside = lax.ppermute(chip, "angle", [(a, a ^ 2) for a in range(angles)])
        total = (chip.astype(jnp.float32) + beside.astype(jnp.float32)) * (1.0 / CHIP_SCALE)
    else:
        groups = [list(range(odd_one, angles, 2)) for odd_one in range(2)]
        total = lax.psum(chip, "angle", axis_index_groups=groups)
    new_rows = (image_rows * total / sens_rows[:, None]).astype(jnp.bfloat16)
    other_rows = lax.ppermute(new_rows, "angle", pairs)
    low = jnp.where(odd == 0, new_rows, other_rows)
    high = jnp.where(odd == 0, other_rows, new_rows)
    return jnp.concatenate([low, high], axis=0)


def solution(mesh):
    placed = (
        P(("groups", "slab"), None),
        P(("groups", "slab")),
        P(("groups", "slab"), "angle", None, None, None),
        P(("groups", "slab"), "angle", None),
        P(("groups", "slab"), "angle", None),
        P(("groups", "slab"), "angle", None),
        P(("groups", "slab"), "angle", None, None),
        P(("groups", "slab"), "angle", None, None),
    )
    return jax.shard_map(
        functools.partial(body, mesh.shape["slab"], mesh.shape["angle"]),
        mesh=mesh,
        in_specs=placed,
        out_specs=P(("groups", "slab"), None),
        check_vma=False,
    )
```

```python
import functools

import jax
import jax.numpy as jnp
from jax import lax
from jax.experimental import pallas as pl
from jax.experimental.pallas import tpu as pltpu
from jax.sharding import PartitionSpec as P

VMEM = pl.BlockSpec(memory_space=pltpu.VMEM)
SMEM = pl.BlockSpec(memory_space=pltpu.SMEM)
HBM = pl.BlockSpec(memory_space=pltpu.HBM)
PART_SCALE = 256.0
CHIP_SCALE = 128.0
GROUP = 4
PIECE = 8


def params(mebibytes=16):
    return pltpu.CompilerParams(vmem_limit_bytes=mebibytes * 1024 * 1024)


def place(slabs):
    slab = lax.axis_index("slab")
    odd = lax.axis_index("angle") % 2
    left = slab > 0
    right = slab < slabs - 1
    even = odd == 0
    forth = jnp.logical_or(jnp.logical_and(even, right), jnp.logical_and(~even, left))
    back = jnp.logical_or(jnp.logical_and(even, left), jnp.logical_and(~even, right))
    return odd, forth, back


def index_tiles(voxel_ref, line_ref, slot_ref, blocks, lines):
    stride = lines + 1
    for n in range(blocks * stride):
        slot_ref[n] = -1
    for k in range(voxel_ref.shape[-1]):
        slot_ref[voxel_ref[k] * stride + line_ref[k]] = k


def tile_of(tiles_ref, slot_ref, voxel, line, lines):
    slot = slot_ref[voxel * (lines + 1) + line]
    tile = tiles_ref[jnp.maximum(slot, 0)]
    return jnp.where(slot >= 0, tile, jnp.zeros_like(tile))


def project(image, tiles_ref, slot_ref, voxels, which, lines):
    weights = jnp.concatenate(
        [
            jnp.concatenate([tile_of(tiles_ref, slot_ref, v, c, lines) for c in which], axis=1)
            for v in voxels
        ],
        axis=0,
    )
    return jnp.dot(image, weights, preferred_element_type=jnp.float32)


def edge_kernel(
    blocks, own, lines, voxel_hbm, line_hbm, activity_hbm, tiles_hbm,
    forth_ref, back_ref, image_ref, tiles_ref,
    voxel_ref, line_ref, activity_ref, slot_ref, small_sem, tile_sem,
):
    size = tiles_ref.shape[-1]
    total = tiles_ref.shape[0]
    width = (lines - own) // 2
    first = [
        pltpu.make_async_copy(voxel_hbm, voxel_ref, small_sem.at[0]),
        pltpu.make_async_copy(line_hbm, line_ref, small_sem.at[1]),
        pltpu.make_async_copy(activity_hbm, activity_ref, small_sem.at[2]),
    ]
    pieces = []
    for n, start in enumerate(range(0, total, PIECE)):
        span = pl.ds(start, min(PIECE, total - start))
        pieces.append(
            pltpu.make_async_copy(tiles_hbm.at[span], tiles_ref.at[span], tile_sem.at[n])
        )
    for copy in first + pieces:
        copy.start()
    first[0].wait()
    first[1].wait()
    index_tiles(voxel_ref, line_ref, slot_ref, blocks, lines)
    first[2].wait()
    for v in range(blocks):
        image_ref[:, v * size : (v + 1) * size] = activity_ref[v * size : (v + 1) * size, :].T
    odd = lax.axis_index("angle") % 2
    outs = (
        (forth_ref, own + width * odd),
        (back_ref, own + width * (1 - odd)),
    )
    sums = [None, None]
    waited = 0
    for low in range(0, blocks, GROUP):
        high = min(low + GROUP, blocks)
        needed = len(pieces) if high == blocks else min(len(pieces), pl.cdiv(high * lines, PIECE))
        for copy in pieces[waited:needed]:
            copy.wait()
        waited = needed
        image = image_ref[:, low * size : high * size]
        for n, (_, start) in enumerate(outs):
            which = [start + c for c in range(width)]
            part = project(image, tiles_ref, slot_ref, range(low, high), which, lines)
            sums[n] = part if sums[n] is None else sums[n] + part
    for n, (out_ref, _) in enumerate(outs):
        for c in range(width):
            out_ref[c] = sums[n][:, c * size : (c + 1) * size].astype(out_ref.dtype)


def own_kernel(
    blocks, own, lines, voxel_ref, line_ref, rows_ref, image_ref, tiles_ref, counts_ref,
    background_ref, base_ref, measured_ref, ratio_ref, matrix_ref, slot_ref, order_ref,
):
    size = tiles_ref.shape[-1]
    width = (lines - own) // 2
    half = blocks // 2
    index_tiles(voxel_ref, line_ref, slot_ref, blocks, lines)
    for j in range(width):
        order_ref[j] = rows_ref[j]
    at = jnp.int32(width)
    for o in range(own):
        oblique = functools.reduce(jnp.logical_or, [rows_ref[j] == o for j in range(width)])
        order_ref[jnp.where(oblique, own, at)] = o
        at = at + jnp.where(oblique, 0, 1)
    image = image_ref[...]
    for start in range(0, own, width):
        which = [order_ref[start + c] for c in range(width)]
        sums = project(image, tiles_ref, slot_ref, range(blocks), which, lines)
        for c, row in enumerate(which):
            base = sums[:, c * size : (c + 1) * size].T + background_ref[row].astype(jnp.float32)
            measured = counts_ref[row].astype(jnp.float32)
            if start == 0:
                base_ref[c] = base
                measured_ref[c] = measured
            else:
                ratio_ref[start - width + c] = (measured / base).astype(ratio_ref.dtype)
    away = (1 - lax.axis_index("angle") % 2) * half
    for v in range(blocks):
        voxel = away + v if v < half else half - away + v - half
        for c in range(lines):
            line = order_ref[c] if c < own else c
            matrix_ref[v * size : (v + 1) * size, c * size : (c + 1) * size] = tile_of(
                tiles_ref, slot_ref, voxel, line, lines
            )


def oblique_kernel(slabs, forth_ref, back_ref, base_ref, measured_ref, out_ref):
    _, has_forth, has_back = place(slabs)
    for j in range(out_ref.shape[0]):
        forth = forth_ref[j].astype(jnp.float32)
        back = back_ref[j].astype(jnp.float32)
        extra = jnp.where(has_forth, forth, 0.0) + jnp.where(has_back, back, 0.0)
        out_ref[j] = (measured_ref[j] / (base_ref[j] + extra.T)).astype(out_ref.dtype)


def own_back_kernel(own, matrix_ref, oblique_ref, ratio_ref, out_ref):
    size = ratio_ref.shape[1]
    ratios = jnp.concatenate([oblique_ref[...], ratio_ref[...]], axis=0)
    ratios = ratios.reshape(own * size, -1)
    out_ref[...] = jnp.dot(
        matrix_ref[:, : own * size], ratios, preferred_element_type=jnp.float32
    )


def edge_back_kernel(slabs, own, start, scale, matrix_ref, forth_ref, back_ref, own_ref, out_ref):
    size = forth_ref.shape[1]
    rows = out_ref.shape[0]
    odd, has_forth, has_back = place(slabs)
    forth = jnp.where(has_forth, forth_ref[...], jnp.zeros_like(forth_ref))
    back = jnp.where(has_back, back_ref[...], jnp.zeros_like(back_ref))
    left = jnp.where(odd == 0, back, forth)
    right = jnp.where(odd == 0, forth, back)
    ratios = jnp.concatenate([left, right], axis=0)
    ratios = ratios.reshape(ratios.shape[0] * size, -1)
    sums = jnp.dot(
        matrix_ref[start : start + rows, own * size :], ratios, preferred_element_type=jnp.float32
    )
    out_ref[...] = (sums + own_ref[start : start + rows]) * scale


def body(
    slabs, angles, activity, sensitivity, system_tiles, tile_voxel, tile_line, oblique_rows,
    counts, background,
):
    size = system_tiles.shape[-1]
    frames = activity.shape[1]
    blocks = activity.shape[0] // size
    own = counts.shape[2] // size
    width = oblique_rows.shape[-1]
    lines = own + 2 * width
    half = blocks // 2
    tiles = system_tiles[0, 0]
    voxel = tile_voxel[0, 0]
    line = tile_line[0, 0]
    rows = oblique_rows[0, 0]
    measured = counts[0, 0].reshape(own, size, frames)
    additive = background[0, 0].reshape(own, size, frames)

    forth = []
    for s in range(slabs):
        for a in range(angles):
            t = s - 1 if a % 2 == 0 else s + 1
            here = s * angles + a
            there = t * angles + a if 0 <= t < slabs else s * angles + (a ^ 1)
            forth.append((here, there))
    back = [(there, here) for here, there in forth]
    both = ("slab", "angle")
    slots = pltpu.SMEM((blocks * (lines + 1),), jnp.int32)

    def array(dtype, *shape):
        return jax.ShapeDtypeStruct(shape, dtype)

    edge_forth, edge_back, image, held = pl.pallas_call(
        functools.partial(edge_kernel, blocks, own, lines),
        out_shape=(
            array(jnp.bfloat16, width, frames, size),
            array(jnp.bfloat16, width, frames, size),
            array(jnp.bfloat16, frames, blocks * size),
            array(jnp.bfloat16, *tiles.shape),
        ),
        in_specs=[HBM] * 4,
        out_specs=(VMEM,) * 4,
        scratch_shapes=[
            pltpu.SMEM(voxel.shape, jnp.int32),
            pltpu.SMEM(line.shape, jnp.int32),
            pltpu.VMEM(activity.shape, activity.dtype),
            slots,
            pltpu.SemaphoreType.DMA((3,)),
            pltpu.SemaphoreType.DMA((pl.cdiv(tiles.shape[0], PIECE),)),
        ],
        compiler_params=params(),
        name="edge_partials",
    )(*[pltpu.with_memory_space_constraint(a, pltpu.HBM) for a in (voxel, line, activity, tiles)])
    got_forth = lax.ppermute(edge_forth, both, forth)
    got_back = lax.ppermute(edge_back, both, back)
    base, taken, ratio, matrix = pl.pallas_call(
        functools.partial(own_kernel, blocks, own, lines),
        out_shape=(
            array(jnp.float32, width, size, frames),
            array(jnp.float32, width, size, frames),
            array(jnp.bfloat16, own - width, size, frames),
            array(jnp.bfloat16, blocks * size, lines * size),
        ),
        in_specs=[SMEM] * 3 + [VMEM] * 4,
        out_specs=(VMEM,) * 4,
        scratch_shapes=[slots, pltpu.SMEM((own + 1,), jnp.int32)],
        compiler_params=params(),
        name="own_partials",
    )(voxel, line, rows, image, held, measured, additive)
    oblique = pl.pallas_call(
        functools.partial(oblique_kernel, slabs),
        out_shape=array(jnp.bfloat16, width, size, frames),
        in_specs=[VMEM] * 4,
        out_specs=VMEM,
        compiler_params=params(),
        name="oblique_ratios",
    )(got_forth, got_back, base, taken)
    beside_forth = lax.ppermute(oblique, both, forth)
    beside_back = lax.ppermute(oblique, both, back)
    own_back = pl.pallas_call(
        functools.partial(own_back_kernel, own),
        out_shape=array(jnp.float32, blocks * size, frames),
        in_specs=[VMEM] * 3,
        out_specs=VMEM,
        compiler_params=params(),
        name="own_back",
    )(matrix, oblique, ratio)

    half_rows = half * size

    def edge_half(start, scale, name):
        return pl.pallas_call(
            functools.partial(edge_back_kernel, slabs, own, start, scale),
            out_shape=array(jnp.float32, half_rows, frames),
            in_specs=[VMEM] * 4,
            out_specs=VMEM,
            compiler_params=params(),
            name=name,
        )(matrix, beside_forth, beside_back, own_back)

    odd = lax.axis_index("angle") % 2
    mine = odd * half_rows
    image_rows = lax.dynamic_slice_in_dim(activity, mine, half_rows, 0).astype(jnp.float32)
    sens_rows = lax.dynamic_slice_in_dim(sensitivity, mine, half_rows, 0)
    gain = image_rows / sens_rows[:, None]
    pairs = [(a, a ^ 1) for a in range(angles)]
    sent = edge_half(0, PART_SCALE, "edge_back_sent").astype(jnp.float16)
    got = lax.ppermute(sent, "angle", pairs)
    kept = edge_half(half_rows, 1.0, "edge_back_kept")
    chip = kept + got.astype(jnp.float32) * (1.0 / PART_SCALE)
    if angles == 4:
        chip = (chip * CHIP_SCALE).astype(jnp.float16)
        beside = lax.ppermute(chip, "angle", [(a, a ^ 2) for a in range(angles)])
        total = (chip.astype(jnp.float32) + beside.astype(jnp.float32)) * (1.0 / CHIP_SCALE)
    else:
        groups = [list(range(odd_one, angles, 2)) for odd_one in range(2)]
        total = lax.psum(chip, "angle", axis_index_groups=groups)
    new_rows = (gain * total).astype(jnp.bfloat16)
    other_rows = lax.ppermute(new_rows, "angle", pairs)
    low = jnp.where(odd == 0, new_rows, other_rows)
    high = jnp.where(odd == 0, other_rows, new_rows)
    return jnp.concatenate([low, high], axis=0)


def solution(mesh):
    placed = (
        P(("groups", "slab"), None),
        P(("groups", "slab")),
        P(("groups", "slab"), "angle", None, None, None),
        P(("groups", "slab"), "angle", None),
        P(("groups", "slab"), "angle", None),
        P(("groups", "slab"), "angle", None),
        P(("groups", "slab"), "angle", None, None),
        P(("groups", "slab"), "angle", None, None),
    )
    return jax.shard_map(
        functools.partial(body, mesh.shape["slab"], mesh.shape["angle"]),
        mesh=mesh,
        in_specs=placed,
        out_specs=P(("groups", "slab"), None),
        check_vma=False,
    )
```

```python
import functools

import jax
import jax.numpy as jnp
from jax import lax
from jax.experimental import pallas as pl
from jax.experimental.pallas import tpu as pltpu
from jax.sharding import PartitionSpec as P

VMEM = pl.BlockSpec(memory_space=pltpu.VMEM)
SMEM = pl.BlockSpec(memory_space=pltpu.SMEM)
HBM = pl.BlockSpec(memory_space=pltpu.HBM)
PART_SCALE = 256.0
CHIP_SCALE = 128.0
GROUP = 4
PIECE = 32


def params(mebibytes=16):
    return pltpu.CompilerParams(vmem_limit_bytes=mebibytes * 1024 * 1024)


def place(slabs):
    slab = lax.axis_index("slab")
    odd = lax.axis_index("angle") % 2
    left = slab > 0
    right = slab < slabs - 1
    even = odd == 0
    forth = jnp.logical_or(jnp.logical_and(even, right), jnp.logical_and(~even, left))
    back = jnp.logical_or(jnp.logical_and(even, left), jnp.logical_and(~even, right))
    return odd, forth, back


def index_tiles(voxel_ref, line_ref, slot_ref, blocks, lines):
    stride = lines + 1
    for n in range(blocks * stride):
        slot_ref[n] = -1
    for k in range(voxel_ref.shape[-1]):
        slot_ref[voxel_ref[k] * stride + line_ref[k]] = k


def tile_of(tiles_ref, slot_ref, voxel, line, lines):
    slot = slot_ref[voxel * (lines + 1) + line]
    tile = tiles_ref[jnp.maximum(slot, 0)]
    return jnp.where(slot >= 0, tile, jnp.zeros_like(tile))


def project(image, tiles_ref, slot_ref, voxels, which, lines):
    weights = jnp.concatenate(
        [
            jnp.concatenate([tile_of(tiles_ref, slot_ref, v, c, lines) for c in which], axis=1)
            for v in voxels
        ],
        axis=0,
    )
    return jnp.dot(image, weights, preferred_element_type=jnp.float32)


def edge_kernel(
    blocks, own, lines, voxel_hbm, line_hbm, activity_hbm, tiles_hbm,
    forth_ref, back_ref, image_ref, tiles_ref,
    voxel_ref, line_ref, activity_ref, slot_ref, small_sem, tile_sem,
):
    size = tiles_ref.shape[-1]
    total = tiles_ref.shape[0]
    width = (lines - own) // 2
    first = [
        pltpu.make_async_copy(voxel_hbm, voxel_ref, small_sem.at[0]),
        pltpu.make_async_copy(line_hbm, line_ref, small_sem.at[1]),
        pltpu.make_async_copy(activity_hbm, activity_ref, small_sem.at[2]),
    ]
    pieces = []
    for n, start in enumerate(range(0, total, PIECE)):
        span = pl.ds(start, min(PIECE, total - start))
        pieces.append(
            pltpu.make_async_copy(tiles_hbm.at[span], tiles_ref.at[span], tile_sem.at[n])
        )
    for copy in first + pieces:
        copy.start()
    first[0].wait()
    first[1].wait()
    index_tiles(voxel_ref, line_ref, slot_ref, blocks, lines)
    first[2].wait()
    for v in range(blocks):
        image_ref[:, v * size : (v + 1) * size] = activity_ref[v * size : (v + 1) * size, :].T
    odd = lax.axis_index("angle") % 2
    outs = (
        (forth_ref, own + width * odd),
        (back_ref, own + width * (1 - odd)),
    )
    sums = [None, None]
    waited = 0
    for low in range(0, blocks, GROUP):
        high = min(low + GROUP, blocks)
        needed = len(pieces) if high == blocks else min(len(pieces), pl.cdiv(high * lines, PIECE))
        for copy in pieces[waited:needed]:
            copy.wait()
        waited = needed
        image = image_ref[:, low * size : high * size]
        for n, (_, start) in enumerate(outs):
            which = [start + c for c in range(width)]
            part = project(image, tiles_ref, slot_ref, range(low, high), which, lines)
            sums[n] = part if sums[n] is None else sums[n] + part
    for n, (out_ref, _) in enumerate(outs):
        for c in range(width):
            out_ref[c] = sums[n][:, c * size : (c + 1) * size].astype(out_ref.dtype)


def own_kernel(
    blocks, own, lines, voxel_ref, line_ref, rows_ref, image_ref, tiles_ref, counts_ref,
    background_ref, base_ref, measured_ref, ratio_ref, matrix_ref, slot_ref, order_ref,
):
    size = tiles_ref.shape[-1]
    width = (lines - own) // 2
    index_tiles(voxel_ref, line_ref, slot_ref, blocks, lines)
    for j in range(width):
        order_ref[j] = rows_ref[j]
    at = jnp.int32(width)
    for o in range(own):
        oblique = functools.reduce(jnp.logical_or, [rows_ref[j] == o for j in range(width)])
        order_ref[jnp.where(oblique, own, at)] = o
        at = at + jnp.where(oblique, 0, 1)
    image = image_ref[...]
    for start in range(0, own, width):
        which = [order_ref[start + c] for c in range(width)]
        sums = project(image, tiles_ref, slot_ref, range(blocks), which, lines)
        for c, row in enumerate(which):
            base = sums[:, c * size : (c + 1) * size].T + background_ref[row].astype(jnp.float32)
            measured = counts_ref[row].astype(jnp.float32)
            if start == 0:
                base_ref[c] = base
                measured_ref[c] = measured
            else:
                ratio_ref[start - width + c] = (measured / base).astype(ratio_ref.dtype)
    away = (1 - lax.axis_index("angle") % 2) * (blocks // 2)
    for v in range(blocks):
        voxel = lax.rem(away + v, blocks)
        for c in range(lines):
            line = order_ref[c] if c < own else c
            matrix_ref[v * size : (v + 1) * size, c * size : (c + 1) * size] = tile_of(
                tiles_ref, slot_ref, voxel, line, lines
            )


def oblique_kernel(slabs, forth_ref, back_ref, base_ref, measured_ref, out_ref):
    _, has_forth, has_back = place(slabs)
    for j in range(out_ref.shape[0]):
        forth = forth_ref[j].astype(jnp.float32)
        back = back_ref[j].astype(jnp.float32)
        extra = jnp.where(has_forth, forth, 0.0) + jnp.where(has_back, back, 0.0)
        out_ref[j] = (measured_ref[j] / (base_ref[j] + extra.T)).astype(out_ref.dtype)


def own_back_kernel(own, matrix_ref, oblique_ref, ratio_ref, out_ref):
    size = ratio_ref.shape[1]
    ratios = jnp.concatenate([oblique_ref[...], ratio_ref[...]], axis=0)
    ratios = ratios.reshape(own * size, -1)
    out_ref[...] = jnp.dot(
        matrix_ref[:, : own * size], ratios, preferred_element_type=jnp.float32
    )


def gain_kernel(size, activity_ref, sensitivity_ref, gain_ref):
    count = gain_ref.shape[0] // size
    first = lax.axis_index("angle") % 2 * count
    for n in range(count):
        at = pl.multiple_of((first + n) * size, size)
        values = activity_ref[pl.ds(at, size)].astype(jnp.float32)
        sens = sensitivity_ref[pl.ds(first + n, 1)]
        gain = values / jnp.broadcast_to(sens, (size, size)).T
        gain_ref[n * size : (n + 1) * size] = gain * (1.0 / CHIP_SCALE)


def edge_back_kernel(slabs, own, start, scale, matrix_ref, forth_ref, back_ref, own_ref, out_ref):
    size = forth_ref.shape[1]
    rows = out_ref.shape[0]
    odd, has_forth, has_back = place(slabs)
    forth = jnp.where(has_forth, forth_ref[...], jnp.zeros_like(forth_ref))
    back = jnp.where(has_back, back_ref[...], jnp.zeros_like(back_ref))
    left = jnp.where(odd == 0, back, forth)
    right = jnp.where(odd == 0, forth, back)
    ratios = jnp.concatenate([left, right], axis=0)
    ratios = ratios.reshape(ratios.shape[0] * size, -1)
    sums = jnp.dot(
        matrix_ref[start : start + rows, own * size :], ratios, preferred_element_type=jnp.float32
    )
    out_ref[...] = (sums + own_ref[start : start + rows]) * scale


def write_rows_kernel(turn, rows_ref, *refs):
    out_hbm, sem = refs[-2:]
    count = rows_ref.shape[0]
    at = pl.multiple_of((lax.axis_index("angle") + turn) % 2 * count, count)
    copy = pltpu.make_async_copy(rows_ref, out_hbm.at[pl.ds(at, count)], sem)
    copy.start()
    copy.wait()


def body(
    slabs, angles, activity, sensitivity, system_tiles, tile_voxel, tile_line, oblique_rows,
    counts, background,
):
    size = system_tiles.shape[-1]
    frames = activity.shape[1]
    blocks = activity.shape[0] // size
    own = counts.shape[2] // size
    width = oblique_rows.shape[-1]
    lines = own + 2 * width
    half = blocks // 2
    tiles = system_tiles[0, 0]
    voxel = tile_voxel[0, 0]
    line = tile_line[0, 0]
    rows = oblique_rows[0, 0]
    measured = counts[0, 0].reshape(own, size, frames)
    additive = background[0, 0].reshape(own, size, frames)

    forth = []
    for s in range(slabs):
        for a in range(angles):
            t = s - 1 if a % 2 == 0 else s + 1
            here = s * angles + a
            there = t * angles + a if 0 <= t < slabs else s * angles + (a ^ 1)
            forth.append((here, there))
    back = [(there, here) for here, there in forth]
    both = ("slab", "angle")
    slots = pltpu.SMEM((blocks * (lines + 1),), jnp.int32)

    def array(dtype, *shape):
        return jax.ShapeDtypeStruct(shape, dtype)

    edge_forth, edge_back, image, held = pl.pallas_call(
        functools.partial(edge_kernel, blocks, own, lines),
        out_shape=(
            array(jnp.bfloat16, width, frames, size),
            array(jnp.bfloat16, width, frames, size),
            array(jnp.bfloat16, frames, blocks * size),
            array(jnp.bfloat16, *tiles.shape),
        ),
        in_specs=[HBM] * 4,
        out_specs=(VMEM,) * 4,
        scratch_shapes=[
            pltpu.SMEM(voxel.shape, jnp.int32),
            pltpu.SMEM(line.shape, jnp.int32),
            pltpu.VMEM(activity.shape, activity.dtype),
            slots,
            pltpu.SemaphoreType.DMA((3,)),
            pltpu.SemaphoreType.DMA((pl.cdiv(tiles.shape[0], PIECE),)),
        ],
        compiler_params=params(),
        name="edge_partials",
    )(*[pltpu.with_memory_space_constraint(a, pltpu.HBM) for a in (voxel, line, activity, tiles)])
    got_forth = lax.ppermute(edge_forth, both, forth)
    got_back = lax.ppermute(edge_back, both, back)
    base, taken, ratio, matrix = pl.pallas_call(
        functools.partial(own_kernel, blocks, own, lines),
        out_shape=(
            array(jnp.float32, width, size, frames),
            array(jnp.float32, width, size, frames),
            array(jnp.bfloat16, own - width, size, frames),
            array(jnp.bfloat16, blocks * size, lines * size),
        ),
        in_specs=[SMEM] * 3 + [VMEM] * 4,
        out_specs=(VMEM,) * 4,
        scratch_shapes=[slots, pltpu.SMEM((own + 1,), jnp.int32)],
        compiler_params=params(),
        name="own_partials",
    )(voxel, line, rows, image, held, measured, additive)
    oblique = pl.pallas_call(
        functools.partial(oblique_kernel, slabs),
        out_shape=array(jnp.bfloat16, width, size, frames),
        in_specs=[VMEM] * 4,
        out_specs=VMEM,
        compiler_params=params(),
        name="oblique_ratios",
    )(got_forth, got_back, base, taken)
    beside_forth = lax.ppermute(oblique, both, forth)
    beside_back = lax.ppermute(oblique, both, back)
    half_rows = half * size
    own_back = pl.pallas_call(
        functools.partial(own_back_kernel, own),
        out_shape=array(jnp.float32, blocks * size, frames),
        in_specs=[VMEM] * 3,
        out_specs=VMEM,
        compiler_params=params(),
        name="own_back",
    )(matrix, oblique, ratio)
    gain = pl.pallas_call(
        functools.partial(gain_kernel, size),
        out_shape=array(jnp.float32, half_rows, frames),
        in_specs=[VMEM] * 2,
        out_specs=VMEM,
        compiler_params=params(),
        name="gain",
    )(activity, sensitivity.reshape(blocks, size))

    def edge_rows(start, scale, name):
        return pl.pallas_call(
            functools.partial(edge_back_kernel, slabs, own, start, scale),
            out_shape=array(jnp.float32, half_rows, frames),
            in_specs=[VMEM] * 4,
            out_specs=VMEM,
            compiler_params=params(),
            name=name,
        )(matrix, beside_forth, beside_back, own_back)

    def wide(values):
        return values.astype(jnp.float32)

    pairs = [(a, a ^ 1) for a in range(angles)]
    away = edge_rows(0, PART_SCALE, "edge_back_sent").astype(jnp.float16)
    got = lax.ppermute(away, "angle", pairs)
    home = edge_rows(half_rows, 1.0, "edge_back_kept")
    chip = (home + wide(got) * (1.0 / PART_SCALE)) * CHIP_SCALE
    if angles == 4:
        chip = lax.optimization_barrier(chip.astype(jnp.float16))
        across = lax.ppermute(chip, "angle", [(a, a ^ 2) for a in range(angles)])
        total = wide(chip) + wide(across)
    else:
        groups = [list(range(odd_one, angles, 2)) for odd_one in range(2)]
        total = lax.psum(chip, "angle", axis_index_groups=groups)
    rows_home = lax.optimization_barrier((gain * total).astype(jnp.bfloat16))
    rows_away = lax.ppermute(rows_home, "angle", pairs)

    def write_rows(turn, name, *inputs):
        return pl.pallas_call(
            functools.partial(write_rows_kernel, turn),
            out_shape=array(jnp.bfloat16, blocks * size, frames),
            in_specs=[VMEM, HBM][: len(inputs)],
            out_specs=HBM,
            scratch_shapes=[pltpu.SemaphoreType.DMA],
            input_output_aliases={1: 0} if len(inputs) > 1 else {},
            compiler_params=params(),
            name=name,
        )(*inputs)

    updated = write_rows(0, "write_home", rows_home)
    return write_rows(1, "write_away", rows_away, updated)


def solution(mesh):
    placed = (
        P(("groups", "slab"), None),
        P(("groups", "slab")),
        P(("groups", "slab"), "angle", None, None, None),
        P(("groups", "slab"), "angle", None),
        P(("groups", "slab"), "angle", None),
        P(("groups", "slab"), "angle", None),
        P(("groups", "slab"), "angle", None, None),
        P(("groups", "slab"), "angle", None, None),
    )
    return jax.shard_map(
        functools.partial(body, mesh.shape["slab"], mesh.shape["angle"]),
        mesh=mesh,
        in_specs=placed,
        out_specs=P(("groups", "slab"), None),
        check_vma=False,
    )
```

```python
import functools

import jax
import jax.numpy as jnp
from jax import lax
from jax.experimental import pallas as pl
from jax.experimental.pallas import tpu as pltpu
from jax.sharding import PartitionSpec as P

VMEM = pl.BlockSpec(memory_space=pltpu.VMEM)
SMEM = pl.BlockSpec(memory_space=pltpu.SMEM)
HBM = pl.BlockSpec(memory_space=pltpu.HBM)
PART_SCALE = 256.0
CHIP_SCALE = 128.0
GROUP = 4
PIECE = 32


def params(mebibytes=16):
    return pltpu.CompilerParams(vmem_limit_bytes=mebibytes * 1024 * 1024)


def place(slabs):
    slab = lax.axis_index("slab")
    odd = lax.axis_index("angle") % 2
    left = slab > 0
    right = slab < slabs - 1
    even = odd == 0
    forth = jnp.logical_or(jnp.logical_and(even, right), jnp.logical_and(~even, left))
    back = jnp.logical_or(jnp.logical_and(even, left), jnp.logical_and(~even, right))
    return odd, forth, back


def index_tiles(voxel_ref, line_ref, slot_ref, blocks, lines):
    stride = lines + 1
    for n in range(blocks * stride):
        slot_ref[n] = -1
    for k in range(voxel_ref.shape[-1]):
        slot_ref[voxel_ref[k] * stride + line_ref[k]] = k


def tile_of(tiles_ref, slot_ref, voxel, line, lines):
    slot = slot_ref[voxel * (lines + 1) + line]
    tile = tiles_ref[jnp.maximum(slot, 0)]
    return jnp.where(slot >= 0, tile, jnp.zeros_like(tile))


def project(image, tiles_ref, slot_ref, voxels, which, lines):
    weights = jnp.concatenate(
        [
            jnp.concatenate([tile_of(tiles_ref, slot_ref, v, c, lines) for c in which], axis=1)
            for v in voxels
        ],
        axis=0,
    )
    return jnp.dot(image, weights, preferred_element_type=jnp.float32)


def edge_kernel(
    blocks, own, lines, voxel_hbm, line_hbm, activity_hbm, tiles_hbm,
    forth_ref, back_ref, image_ref, tiles_ref,
    voxel_ref, line_ref, activity_ref, slot_ref, small_sem, tile_sem,
):
    size = tiles_ref.shape[-1]
    total = tiles_ref.shape[0]
    width = (lines - own) // 2
    first = [
        pltpu.make_async_copy(voxel_hbm, voxel_ref, small_sem.at[0]),
        pltpu.make_async_copy(line_hbm, line_ref, small_sem.at[1]),
        pltpu.make_async_copy(activity_hbm, activity_ref, small_sem.at[2]),
    ]
    pieces = []
    for n, start in enumerate(range(0, total, PIECE)):
        span = pl.ds(start, min(PIECE, total - start))
        pieces.append(
            pltpu.make_async_copy(tiles_hbm.at[span], tiles_ref.at[span], tile_sem.at[n])
        )
    for copy in first:
        copy.start()
    for copy in pieces:
        copy.start(priority=1)
    first[0].wait()
    first[1].wait()
    index_tiles(voxel_ref, line_ref, slot_ref, blocks, lines)
    first[2].wait()
    for v in range(blocks):
        image_ref[:, v * size : (v + 1) * size] = activity_ref[v * size : (v + 1) * size, :].T
    odd = lax.axis_index("angle") % 2
    outs = (
        (forth_ref, own + width * odd),
        (back_ref, own + width * (1 - odd)),
    )
    sums = [None, None]
    waited = 0
    for low in range(0, blocks, GROUP):
        high = min(low + GROUP, blocks)
        needed = len(pieces) if high == blocks else min(len(pieces), pl.cdiv(high * lines, PIECE))
        for copy in pieces[waited:needed]:
            copy.wait()
        waited = needed
        image = image_ref[:, low * size : high * size]
        for n, (_, start) in enumerate(outs):
            which = [start + c for c in range(width)]
            part = project(image, tiles_ref, slot_ref, range(low, high), which, lines)
            sums[n] = part if sums[n] is None else sums[n] + part
    for n, (out_ref, _) in enumerate(outs):
        for c in range(width):
            out_ref[c] = sums[n][:, c * size : (c + 1) * size].astype(out_ref.dtype)


def own_kernel(
    blocks, own, lines, voxel_ref, line_ref, rows_ref, image_ref, tiles_ref, counts_ref,
    background_ref, base_ref, measured_ref, ratio_ref, matrix_ref, slot_ref, order_ref,
):
    size = tiles_ref.shape[-1]
    width = (lines - own) // 2
    index_tiles(voxel_ref, line_ref, slot_ref, blocks, lines)
    for j in range(width):
        order_ref[j] = rows_ref[j]
    at = jnp.int32(width)
    for o in range(own):
        oblique = functools.reduce(jnp.logical_or, [rows_ref[j] == o for j in range(width)])
        order_ref[jnp.where(oblique, own, at)] = o
        at = at + jnp.where(oblique, 0, 1)
    image = image_ref[...]
    for start in range(0, own, width):
        which = [order_ref[start + c] for c in range(width)]
        sums = project(image, tiles_ref, slot_ref, range(blocks), which, lines)
        for c, row in enumerate(which):
            base = sums[:, c * size : (c + 1) * size].T + background_ref[row].astype(jnp.float32)
            measured = counts_ref[row].astype(jnp.float32)
            if start == 0:
                base_ref[c] = base
                measured_ref[c] = measured
            else:
                ratio_ref[start - width + c] = (measured / base).astype(ratio_ref.dtype)
    away = (1 - lax.axis_index("angle") % 2) * (blocks // 2)
    for v in range(blocks):
        voxel = lax.rem(away + v, blocks)
        for c in range(lines):
            line = order_ref[c] if c < own else c
            matrix_ref[v * size : (v + 1) * size, c * size : (c + 1) * size] = tile_of(
                tiles_ref, slot_ref, voxel, line, lines
            )


def oblique_kernel(slabs, forth_ref, back_ref, base_ref, measured_ref, out_ref):
    _, has_forth, has_back = place(slabs)
    for j in range(out_ref.shape[0]):
        forth = forth_ref[j].astype(jnp.float32)
        back = back_ref[j].astype(jnp.float32)
        extra = jnp.where(has_forth, forth, 0.0) + jnp.where(has_back, back, 0.0)
        out_ref[j] = (measured_ref[j] / (base_ref[j] + extra.T)).astype(out_ref.dtype)


def own_back_kernel(own, matrix_ref, oblique_ref, ratio_ref, out_ref):
    size = ratio_ref.shape[1]
    ratios = jnp.concatenate([oblique_ref[...], ratio_ref[...]], axis=0)
    ratios = ratios.reshape(own * size, -1)
    out_ref[...] = jnp.dot(
        matrix_ref[:, : own * size], ratios, preferred_element_type=jnp.float32
    )


def gain_kernel(size, activity_ref, sensitivity_ref, gain_ref):
    count = gain_ref.shape[0] // size
    first = lax.axis_index("angle") % 2 * count
    for n in range(count):
        at = pl.multiple_of((first + n) * size, size)
        values = activity_ref[pl.ds(at, size)].astype(jnp.float32)
        sens = sensitivity_ref[pl.ds(first + n, 1)]
        gain = values / jnp.broadcast_to(sens, (size, size)).T
        gain_ref[n * size : (n + 1) * size] = gain * (1.0 / CHIP_SCALE)


def edge_back_kernel(slabs, own, start, scale, matrix_ref, forth_ref, back_ref, own_ref, out_ref):
    size = forth_ref.shape[1]
    rows = out_ref.shape[0]
    odd, has_forth, has_back = place(slabs)
    forth = jnp.where(has_forth, forth_ref[...], jnp.zeros_like(forth_ref))
    back = jnp.where(has_back, back_ref[...], jnp.zeros_like(back_ref))
    left = jnp.where(odd == 0, back, forth)
    right = jnp.where(odd == 0, forth, back)
    ratios = jnp.concatenate([left, right], axis=0)
    ratios = ratios.reshape(ratios.shape[0] * size, -1)
    sums = jnp.dot(
        matrix_ref[start : start + rows, own * size :], ratios, preferred_element_type=jnp.float32
    )
    out_ref[...] = (sums + own_ref[start : start + rows]) * scale


def write_rows_kernel(half_rows, places, *refs):
    out_hbm, sem = refs[-2:]
    odd = lax.axis_index("angle") % 2
    copies = []
    for n, (turn, start) in enumerate(places):
        count = refs[n].shape[0]
        at = pl.multiple_of((odd + turn) % 2 * half_rows + start, 128)
        copies.append(
            pltpu.make_async_copy(refs[n], out_hbm.at[pl.ds(at, count)], sem.at[n])
        )
    for copy in copies:
        copy.start()
    for copy in copies:
        copy.wait()


def body(
    slabs, angles, activity, sensitivity, system_tiles, tile_voxel, tile_line, oblique_rows,
    counts, background,
):
    size = system_tiles.shape[-1]
    frames = activity.shape[1]
    blocks = activity.shape[0] // size
    own = counts.shape[2] // size
    width = oblique_rows.shape[-1]
    lines = own + 2 * width
    half = blocks // 2
    tiles = system_tiles[0, 0]
    voxel = tile_voxel[0, 0]
    line = tile_line[0, 0]
    rows = oblique_rows[0, 0]
    measured = counts[0, 0].reshape(own, size, frames)
    additive = background[0, 0].reshape(own, size, frames)

    forth = []
    for s in range(slabs):
        for a in range(angles):
            t = s - 1 if a % 2 == 0 else s + 1
            here = s * angles + a
            there = t * angles + a if 0 <= t < slabs else s * angles + (a ^ 1)
            forth.append((here, there))
    back = [(there, here) for here, there in forth]
    both = ("slab", "angle")
    slots = pltpu.SMEM((blocks * (lines + 1),), jnp.int32)

    def array(dtype, *shape):
        return jax.ShapeDtypeStruct(shape, dtype)

    edge_forth, edge_back, image, held = pl.pallas_call(
        functools.partial(edge_kernel, blocks, own, lines),
        out_shape=(
            array(jnp.bfloat16, width, frames, size),
            array(jnp.bfloat16, width, frames, size),
            array(jnp.bfloat16, frames, blocks * size),
            array(jnp.bfloat16, *tiles.shape),
        ),
        in_specs=[HBM] * 4,
        out_specs=(VMEM,) * 4,
        scratch_shapes=[
            pltpu.SMEM(voxel.shape, jnp.int32),
            pltpu.SMEM(line.shape, jnp.int32),
            pltpu.VMEM(activity.shape, activity.dtype),
            slots,
            pltpu.SemaphoreType.DMA((3,)),
            pltpu.SemaphoreType.DMA((pl.cdiv(tiles.shape[0], PIECE),)),
        ],
        compiler_params=params(),
        name="edge_partials",
    )(*[pltpu.with_memory_space_constraint(a, pltpu.HBM) for a in (voxel, line, activity, tiles)])
    got_forth = lax.ppermute(edge_forth, both, forth)
    got_back = lax.ppermute(edge_back, both, back)
    base, taken, ratio, matrix = pl.pallas_call(
        functools.partial(own_kernel, blocks, own, lines),
        out_shape=(
            array(jnp.float32, width, size, frames),
            array(jnp.float32, width, size, frames),
            array(jnp.bfloat16, own - width, size, frames),
            array(jnp.bfloat16, blocks * size, lines * size),
        ),
        in_specs=[SMEM] * 3 + [VMEM] * 4,
        out_specs=(VMEM,) * 4,
        scratch_shapes=[slots, pltpu.SMEM((own + 1,), jnp.int32)],
        compiler_params=params(),
        name="own_partials",
    )(voxel, line, rows, image, held, measured, additive)
    oblique = pl.pallas_call(
        functools.partial(oblique_kernel, slabs),
        out_shape=array(jnp.bfloat16, width, size, frames),
        in_specs=[VMEM] * 4,
        out_specs=VMEM,
        compiler_params=params(),
        name="oblique_ratios",
    )(got_forth, got_back, base, taken)
    beside_forth = lax.ppermute(oblique, both, forth)
    beside_back = lax.ppermute(oblique, both, back)
    half_rows = half * size
    own_back = pl.pallas_call(
        functools.partial(own_back_kernel, own),
        out_shape=array(jnp.float32, blocks * size, frames),
        in_specs=[VMEM] * 3,
        out_specs=VMEM,
        compiler_params=params(),
        name="own_back",
    )(matrix, oblique, ratio)
    gain = pl.pallas_call(
        functools.partial(gain_kernel, size),
        out_shape=array(jnp.float32, half_rows, frames),
        in_specs=[VMEM] * 2,
        out_specs=VMEM,
        compiler_params=params(),
        name="gain",
    )(activity, sensitivity.reshape(blocks, size))

    def edge_rows(start, count, scale, name):
        return pl.pallas_call(
            functools.partial(edge_back_kernel, slabs, own, start, scale),
            out_shape=array(jnp.float32, count, frames),
            in_specs=[VMEM] * 4,
            out_specs=VMEM,
            compiler_params=params(),
            name=name,
        )(matrix, beside_forth, beside_back, own_back)

    def wide(values):
        return values.astype(jnp.float32)

    def write_rows(image_now, name, *parts):
        values = [part[0] for part in parts]
        places = [part[1:] for part in parts]
        before = [] if image_now is None else [image_now]
        return pl.pallas_call(
            functools.partial(write_rows_kernel, half_rows, places),
            out_shape=array(jnp.bfloat16, blocks * size, frames),
            in_specs=[VMEM] * len(values) + [HBM] * len(before),
            out_specs=HBM,
            scratch_shapes=[pltpu.SemaphoreType.DMA((len(values),))],
            input_output_aliases={len(values): 0} if before else {},
            compiler_params=params(),
            name=name,
        )(*values, *before)

    pairs = [(a, a ^ 1) for a in range(angles)]
    cuts = [0, half_rows // 3, half_rows]
    away = edge_rows(0, half_rows, PART_SCALE, "edge_back_sent")
    got = lax.ppermute(away.astype(jnp.float16), "angle", pairs)
    home = edge_rows(half_rows, half_rows, 1.0, "edge_back_kept")
    updated = None
    for n, (at, end) in enumerate(zip(cuts[:-1], cuts[1:])):
        span = slice(at, end)
        chip = (home[span] + wide(got[span]) * (1.0 / PART_SCALE)) * CHIP_SCALE
        if angles == 4:
            chip = lax.optimization_barrier(chip.astype(jnp.float16))
            across = lax.ppermute(chip, "angle", [(a, a ^ 2) for a in range(angles)])
            if updated is not None:
                across, updated = lax.optimization_barrier((across, updated))
            total = wide(chip) + wide(across)
        else:
            groups = [list(range(odd_one, angles, 2)) for odd_one in range(2)]
            total = lax.psum(chip, "angle", axis_index_groups=groups)
        rows_home = (gain[span] * total).astype(jnp.bfloat16)
        rows_home = lax.optimization_barrier(rows_home)
        rows_away = lax.ppermute(rows_home, "angle", pairs)
        if end < half_rows:
            updated = write_rows(updated, f"write_{n}", (rows_home, 0, at), (rows_away, 1, at))
        else:
            updated = write_rows(updated, "write_home", (rows_home, 0, at))
            updated = write_rows(updated, "write_away", (rows_away, 1, at))
    return updated


def solution(mesh):
    placed = (
        P(("groups", "slab"), None),
        P(("groups", "slab")),
        P(("groups", "slab"), "angle", None, None, None),
        P(("groups", "slab"), "angle", None),
        P(("groups", "slab"), "angle", None),
        P(("groups", "slab"), "angle", None),
        P(("groups", "slab"), "angle", None, None),
        P(("groups", "slab"), "angle", None, None),
    )
    return jax.shard_map(
        functools.partial(body, mesh.shape["slab"], mesh.shape["angle"]),
        mesh=mesh,
        in_specs=placed,
        out_specs=P(("groups", "slab"), None),
        check_vma=False,
    )
```

```python
import functools

import jax
import jax.numpy as jnp
from jax import lax
from jax.experimental import pallas as pl
from jax.experimental.pallas import tpu as pltpu
from jax.sharding import PartitionSpec as P

VMEM = pl.BlockSpec(memory_space=pltpu.VMEM)
SMEM = pl.BlockSpec(memory_space=pltpu.SMEM)
HBM = pl.BlockSpec(memory_space=pltpu.HBM)
PART_SCALE = 256.0
CHIP_SCALE = 128.0
GROUP = 4
PIECE = 32
FIRST_PART = 11


def params(mebibytes=16):
    return pltpu.CompilerParams(vmem_limit_bytes=mebibytes * 1024 * 1024)


def place(slabs):
    slab = lax.axis_index("slab")
    odd = lax.axis_index("angle") % 2
    left = slab > 0
    right = slab < slabs - 1
    even = odd == 0
    forth = jnp.logical_or(jnp.logical_and(even, right), jnp.logical_and(~even, left))
    back = jnp.logical_or(jnp.logical_and(even, left), jnp.logical_and(~even, right))
    return odd, forth, back


def index_tiles(voxel_ref, line_ref, slot_ref, blocks, lines):
    stride = lines + 1
    for n in range(blocks * stride):
        slot_ref[n] = -1
    for k in range(voxel_ref.shape[-1]):
        slot_ref[voxel_ref[k] * stride + line_ref[k]] = k


def tile_of(tiles_ref, slot_ref, voxel, line, lines):
    slot = slot_ref[voxel * (lines + 1) + line]
    tile = tiles_ref[jnp.maximum(slot, 0)]
    return jnp.where(slot >= 0, tile, jnp.zeros_like(tile))


def project(image, tiles_ref, slot_ref, voxels, which, lines):
    weights = jnp.concatenate(
        [
            jnp.concatenate([tile_of(tiles_ref, slot_ref, v, c, lines) for c in which], axis=1)
            for v in voxels
        ],
        axis=0,
    )
    return jnp.dot(image, weights, preferred_element_type=jnp.float32)


def edge_kernel(
    blocks, own, lines, voxel_hbm, line_hbm, activity_hbm, tiles_hbm,
    forth_ref, back_ref, image_ref, tiles_ref,
    voxel_ref, line_ref, activity_ref, slot_ref, small_sem, tile_sem,
):
    size = tiles_ref.shape[-1]
    total = tiles_ref.shape[0]
    width = (lines - own) // 2
    first = [
        pltpu.make_async_copy(voxel_hbm, voxel_ref, small_sem.at[0]),
        pltpu.make_async_copy(line_hbm, line_ref, small_sem.at[1]),
        pltpu.make_async_copy(activity_hbm, activity_ref, small_sem.at[2]),
    ]
    pieces = []
    for n, start in enumerate(range(0, total, PIECE)):
        span = pl.ds(start, min(PIECE, total - start))
        pieces.append(
            pltpu.make_async_copy(tiles_hbm.at[span], tiles_ref.at[span], tile_sem.at[n])
        )
    for copy in first:
        copy.start()
    for copy in pieces:
        copy.start(priority=1)
    first[0].wait()
    first[1].wait()
    index_tiles(voxel_ref, line_ref, slot_ref, blocks, lines)
    first[2].wait()
    for v in range(blocks):
        image_ref[:, v * size : (v + 1) * size] = activity_ref[v * size : (v + 1) * size, :].T
    odd = lax.axis_index("angle") % 2
    outs = (
        (forth_ref, own + width * odd),
        (back_ref, own + width * (1 - odd)),
    )
    sums = [None, None]
    waited = 0
    for low in range(0, blocks, GROUP):
        high = min(low + GROUP, blocks)
        needed = len(pieces) if high == blocks else min(len(pieces), pl.cdiv(high * lines, PIECE))
        for copy in pieces[waited:needed]:
            copy.wait()
        waited = needed
        image = image_ref[:, low * size : high * size]
        for n, (_, start) in enumerate(outs):
            which = [start + c for c in range(width)]
            part = project(image, tiles_ref, slot_ref, range(low, high), which, lines)
            sums[n] = part if sums[n] is None else sums[n] + part
    for n, (out_ref, _) in enumerate(outs):
        for c in range(width):
            out_ref[c] = sums[n][:, c * size : (c + 1) * size].astype(out_ref.dtype)


def own_kernel(
    blocks, own, lines, voxel_ref, line_ref, rows_ref, image_ref, tiles_ref, counts_ref,
    background_ref, activity_ref, sensitivity_ref, base_ref, measured_ref, ratio_ref, matrix_ref,
    gain_ref, slot_ref, order_ref,
):
    size = tiles_ref.shape[-1]
    width = (lines - own) // 2
    index_tiles(voxel_ref, line_ref, slot_ref, blocks, lines)
    for j in range(width):
        order_ref[j] = rows_ref[j]
    at = jnp.int32(width)
    for o in range(own):
        oblique = functools.reduce(jnp.logical_or, [rows_ref[j] == o for j in range(width)])
        order_ref[jnp.where(oblique, own, at)] = o
        at = at + jnp.where(oblique, 0, 1)
    image = image_ref[...]
    for start in range(0, own, width):
        which = [order_ref[start + c] for c in range(width)]
        sums = project(image, tiles_ref, slot_ref, range(blocks), which, lines)
        for c, row in enumerate(which):
            base = sums[:, c * size : (c + 1) * size].T + background_ref[row].astype(jnp.float32)
            measured = counts_ref[row].astype(jnp.float32)
            if start == 0:
                base_ref[c] = base
                measured_ref[c] = measured
            else:
                ratio_ref[start - width + c] = (measured / base).astype(ratio_ref.dtype)
    away = (1 - lax.axis_index("angle") % 2) * (blocks // 2)
    for v in range(blocks):
        voxel = lax.rem(away + v, blocks)
        for c in range(lines):
            line = order_ref[c] if c < own else c
            matrix_ref[v * size : (v + 1) * size, c * size : (c + 1) * size] = tile_of(
                tiles_ref, slot_ref, voxel, line, lines
            )
    fill_gain(size, activity_ref, sensitivity_ref, gain_ref)


def oblique_kernel(slabs, forth_ref, back_ref, base_ref, measured_ref, out_ref):
    _, has_forth, has_back = place(slabs)
    for j in range(out_ref.shape[0]):
        forth = forth_ref[j].astype(jnp.float32)
        back = back_ref[j].astype(jnp.float32)
        extra = jnp.where(has_forth, forth, 0.0) + jnp.where(has_back, back, 0.0)
        out_ref[j] = (measured_ref[j] / (base_ref[j] + extra.T)).astype(out_ref.dtype)


def own_back_kernel(own, matrix_ref, oblique_ref, ratio_ref, out_ref):
    size = ratio_ref.shape[1]
    ratios = jnp.concatenate([oblique_ref[...], ratio_ref[...]], axis=0)
    ratios = ratios.reshape(own * size, -1)
    out_ref[...] = jnp.dot(
        matrix_ref[:, : own * size], ratios, preferred_element_type=jnp.float32
    )


def fill_gain(size, activity_ref, sensitivity_ref, gain_ref):
    count = gain_ref.shape[0] // size
    first = lax.axis_index("angle") % 2 * count
    for n in range(count):
        at = pl.multiple_of((first + n) * size, size)
        values = activity_ref[pl.ds(at, size)].astype(jnp.float32)
        sens = sensitivity_ref[pl.ds(first + n, 1)]
        gain = values / jnp.broadcast_to(sens, (size, size)).T
        gain_ref[n * size : (n + 1) * size] = gain * (1.0 / CHIP_SCALE)


def edge_back_kernel(slabs, own, start, scale, matrix_ref, back_ref, forth_ref, own_ref, out_ref):
    size = forth_ref.shape[1]
    rows = out_ref.shape[0]
    odd, has_forth, has_back = place(slabs)
    forth = jnp.where(has_forth, forth_ref[...], jnp.zeros_like(forth_ref))
    back = jnp.where(has_back, back_ref[...], jnp.zeros_like(back_ref))
    left = jnp.where(odd == 0, back, forth)
    right = jnp.where(odd == 0, forth, back)
    ratios = jnp.concatenate([left, right], axis=0)
    ratios = ratios.reshape(ratios.shape[0] * size, -1)
    sums = jnp.dot(
        matrix_ref[start : start + rows, own * size :], ratios, preferred_element_type=jnp.float32
    )
    out_ref[...] = (sums + own_ref[start : start + rows]) * scale


def write_rows_kernel(half_rows, places, *refs):
    out_hbm, sem = refs[-2:]
    odd = lax.axis_index("angle") % 2
    copies = []
    for n, (turn, start) in enumerate(places):
        count = refs[n].shape[0]
        at = pl.multiple_of((odd + turn) % 2 * half_rows + start, 32)
        copies.append(
            pltpu.make_async_copy(refs[n], out_hbm.at[pl.ds(at, count)], sem.at[n])
        )
    for copy in copies:
        copy.start()
    for copy in copies:
        copy.wait()


def body(
    slabs, angles, activity, sensitivity, system_tiles, tile_voxel, tile_line, oblique_rows,
    counts, background,
):
    size = system_tiles.shape[-1]
    frames = activity.shape[1]
    blocks = activity.shape[0] // size
    own = counts.shape[2] // size
    width = oblique_rows.shape[-1]
    lines = own + 2 * width
    half = blocks // 2
    tiles = system_tiles[0, 0]
    voxel = tile_voxel[0, 0]
    line = tile_line[0, 0]
    rows = oblique_rows[0, 0]
    measured = counts[0, 0].reshape(own, size, frames)
    additive = background[0, 0].reshape(own, size, frames)

    forth = []
    for s in range(slabs):
        for a in range(angles):
            t = s - 1 if a % 2 == 0 else s + 1
            here = s * angles + a
            there = t * angles + a if 0 <= t < slabs else s * angles + (a ^ 1)
            forth.append((here, there))
    back = [(there, here) for here, there in forth]
    both = ("slab", "angle")
    slots = pltpu.SMEM((blocks * (lines + 1),), jnp.int32)

    def array(dtype, *shape):
        return jax.ShapeDtypeStruct(shape, dtype)

    edge_forth, edge_back, image, held = pl.pallas_call(
        functools.partial(edge_kernel, blocks, own, lines),
        out_shape=(
            array(jnp.bfloat16, width, frames, size),
            array(jnp.bfloat16, width, frames, size),
            array(jnp.bfloat16, frames, blocks * size),
            array(jnp.bfloat16, *tiles.shape),
        ),
        in_specs=[HBM] * 4,
        out_specs=(VMEM,) * 4,
        scratch_shapes=[
            pltpu.SMEM(voxel.shape, jnp.int32),
            pltpu.SMEM(line.shape, jnp.int32),
            pltpu.VMEM(activity.shape, activity.dtype),
            slots,
            pltpu.SemaphoreType.DMA((3,)),
            pltpu.SemaphoreType.DMA((pl.cdiv(tiles.shape[0], PIECE),)),
        ],
        compiler_params=params(),
        name="edge_partials",
    )(*[pltpu.with_memory_space_constraint(a, pltpu.HBM) for a in (voxel, line, activity, tiles)])
    got_forth = lax.ppermute(edge_forth, both, forth)
    got_back = lax.ppermute(edge_back, both, back)
    half_rows = half * size
    base, taken, ratio, matrix, gain = pl.pallas_call(
        functools.partial(own_kernel, blocks, own, lines),
        out_shape=(
            array(jnp.float32, width, size, frames),
            array(jnp.float32, width, size, frames),
            array(jnp.bfloat16, own - width, size, frames),
            array(jnp.bfloat16, blocks * size, lines * size),
            array(jnp.float32, half_rows, frames),
        ),
        in_specs=[SMEM] * 3 + [VMEM] * 6,
        out_specs=(VMEM,) * 5,
        scratch_shapes=[slots, pltpu.SMEM((own + 1,), jnp.int32)],
        compiler_params=params(),
        name="own_partials",
    )(
        voxel, line, rows, image, held, measured, additive, activity,
        sensitivity.reshape(blocks, size),
    )
    oblique = pl.pallas_call(
        functools.partial(oblique_kernel, slabs),
        out_shape=array(jnp.bfloat16, width, size, frames),
        in_specs=[VMEM] * 4,
        out_specs=VMEM,
        compiler_params=params(),
        name="oblique_ratios",
    )(got_forth, got_back, base, taken)
    beside_forth = lax.ppermute(oblique, both, forth)
    beside_back = lax.ppermute(oblique, both, back)
    own_back = pl.pallas_call(
        functools.partial(own_back_kernel, own),
        out_shape=array(jnp.float32, blocks * size, frames),
        in_specs=[VMEM] * 3,
        out_specs=VMEM,
        compiler_params=params(),
        name="own_back",
    )(matrix, oblique, ratio)

    def edge_rows(start, count, scale, name, after=None):
        return pl.pallas_call(
            functools.partial(edge_back_kernel, slabs, own, start, scale),
            out_shape=array(jnp.float32, count, frames),
            in_specs=[VMEM] * 4,
            out_specs=VMEM,
            compiler_params=params(),
            name=name,
        )(matrix, beside_back if after is None else after, beside_forth, own_back)

    def wide(values):
        return values.astype(jnp.float32)

    def write_rows(image_now, name, *parts):
        values = [part[0] for part in parts]
        places = [part[1:] for part in parts]
        before = [] if image_now is None else [image_now]
        return pl.pallas_call(
            functools.partial(write_rows_kernel, half_rows, places),
            out_shape=array(jnp.bfloat16, blocks * size, frames),
            in_specs=[VMEM] * len(values) + [HBM] * len(before),
            out_specs=HBM,
            scratch_shapes=[pltpu.SemaphoreType.DMA((len(values),))],
            input_output_aliases={len(values): 0} if before else {},
            compiler_params=params(),
            name=name,
        )(*values, *before)

    pairs = [(a, a ^ 1) for a in range(angles)]
    cuts = [0, FIRST_PART * half_rows // 24, half_rows]
    cuts = [0, FIRST_PART * half_rows // 24, half_rows]
    spans = [slice(at, end) for at, end in zip(cuts[:-1], cuts[1:])]
    got = []
    for n, span in enumerate(spans):
        away = edge_rows(span.start, span.stop - span.start, PART_SCALE, f"edge_back_sent_{n}")
        got.append(lax.ppermute(away.astype(jnp.float16), "angle", pairs))
    updated = None
    for n, (at, end) in enumerate(zip(cuts[:-1], cuts[1:])):
        span = spans[n]
        after, got[n] = lax.optimization_barrier((beside_back, got[n])) if n else (None, got[n])
        home = edge_rows(half_rows + at, end - at, 1.0, f"edge_back_kept_{n}", after)
        chip = (home + wide(got[n]) * (1.0 / PART_SCALE)) * CHIP_SCALE
        if angles == 4:
            chip = lax.optimization_barrier(chip.astype(jnp.float16))
            across = lax.ppermute(chip, "angle", [(a, a ^ 2) for a in range(angles)])
            if updated is not None:
                across, updated = lax.optimization_barrier((across, updated))
            total = wide(chip) + wide(across)
        else:
            groups = [list(range(odd_one, angles, 2)) for odd_one in range(2)]
            total = lax.psum(chip, "angle", axis_index_groups=groups)
        rows_home = (gain[span] * total).astype(jnp.bfloat16)
        rows_home = lax.optimization_barrier(rows_home)
        rows_away = lax.ppermute(rows_home, "angle", pairs)
        if end < half_rows:
            updated = write_rows(updated, f"write_{n}", (rows_home, 0, at), (rows_away, 1, at))
        else:
            updated = write_rows(updated, "write_home", (rows_home, 0, at))
            updated = write_rows(updated, "write_away", (rows_away, 1, at))
    return updated


def solution(mesh):
    placed = (
        P(("groups", "slab"), None),
        P(("groups", "slab")),
        P(("groups", "slab"), "angle", None, None, None),
        P(("groups", "slab"), "angle", None),
        P(("groups", "slab"), "angle", None),
        P(("groups", "slab"), "angle", None),
        P(("groups", "slab"), "angle", None, None),
        P(("groups", "slab"), "angle", None, None),
    )
    return jax.shard_map(
        functools.partial(body, mesh.shape["slab"], mesh.shape["angle"]),
        mesh=mesh,
        in_specs=placed,
        out_specs=P(("groups", "slab"), None),
        check_vma=False,
    )
```

```python
import functools

import jax
import jax.numpy as jnp
from jax import lax
from jax.experimental import pallas as pl
from jax.experimental.pallas import tpu as pltpu
from jax.sharding import PartitionSpec as P

VMEM = pl.BlockSpec(memory_space=pltpu.VMEM)
SMEM = pl.BlockSpec(memory_space=pltpu.SMEM)
HBM = pl.BlockSpec(memory_space=pltpu.HBM)
PART_SCALE = 256.0
CHIP_SCALE = 128.0
GROUP = 4
PIECE = 32
FIRST_PART = 11


def params(mebibytes=16):
    return pltpu.CompilerParams(vmem_limit_bytes=mebibytes * 1024 * 1024)


def place(slabs):
    slab = lax.axis_index("slab")
    odd = lax.axis_index("angle") % 2
    left = slab > 0
    right = slab < slabs - 1
    even = odd == 0
    forth = jnp.logical_or(jnp.logical_and(even, right), jnp.logical_and(~even, left))
    back = jnp.logical_or(jnp.logical_and(even, left), jnp.logical_and(~even, right))
    return odd, forth, back


def home_half():
    angle = lax.axis_index("angle")
    return (angle + angle // 2) % 2


def index_tiles(voxel_ref, line_ref, slot_ref, blocks, lines):
    stride = lines + 1
    for n in range(blocks * stride):
        slot_ref[n] = -1
    for k in range(voxel_ref.shape[-1]):
        slot_ref[voxel_ref[k] * stride + line_ref[k]] = k


def tile_of(tiles_ref, slot_ref, voxel, line, lines):
    slot = slot_ref[voxel * (lines + 1) + line]
    tile = tiles_ref[jnp.maximum(slot, 0)]
    return jnp.where(slot >= 0, tile, jnp.zeros_like(tile))


def project(image, tiles_ref, slot_ref, voxels, which, lines):
    weights = jnp.concatenate(
        [
            jnp.concatenate([tile_of(tiles_ref, slot_ref, v, c, lines) for c in which], axis=1)
            for v in voxels
        ],
        axis=0,
    )
    return jnp.dot(image, weights, preferred_element_type=jnp.float32)


def edge_kernel(
    blocks, own, lines, voxel_hbm, line_hbm, activity_hbm, tiles_hbm,
    forth_ref, back_ref, image_ref, tiles_ref,
    voxel_ref, line_ref, activity_ref, slot_ref, small_sem, tile_sem,
):
    size = tiles_ref.shape[-1]
    total = tiles_ref.shape[0]
    width = (lines - own) // 2
    first = [
        pltpu.make_async_copy(voxel_hbm, voxel_ref, small_sem.at[0]),
        pltpu.make_async_copy(line_hbm, line_ref, small_sem.at[1]),
        pltpu.make_async_copy(activity_hbm, activity_ref, small_sem.at[2]),
    ]
    pieces = []
    for n, start in enumerate(range(0, total, PIECE)):
        span = pl.ds(start, min(PIECE, total - start))
        pieces.append(
            pltpu.make_async_copy(tiles_hbm.at[span], tiles_ref.at[span], tile_sem.at[n])
        )
    for copy in first:
        copy.start()
    for copy in pieces:
        copy.start(priority=1)
    first[0].wait()
    first[1].wait()
    index_tiles(voxel_ref, line_ref, slot_ref, blocks, lines)
    first[2].wait()
    for v in range(blocks):
        image_ref[:, v * size : (v + 1) * size] = activity_ref[v * size : (v + 1) * size, :].T
    odd = lax.axis_index("angle") % 2
    outs = (
        (forth_ref, own + width * odd),
        (back_ref, own + width * (1 - odd)),
    )
    sums = [None, None]
    waited = 0
    for low in range(0, blocks, GROUP):
        high = min(low + GROUP, blocks)
        needed = len(pieces) if high == blocks else min(len(pieces), pl.cdiv(high * lines, PIECE))
        for copy in pieces[waited:needed]:
            copy.wait()
        waited = needed
        image = image_ref[:, low * size : high * size]
        for n, (_, start) in enumerate(outs):
            which = [start + c for c in range(width)]
            part = project(image, tiles_ref, slot_ref, range(low, high), which, lines)
            sums[n] = part if sums[n] is None else sums[n] + part
    for n, (out_ref, _) in enumerate(outs):
        for c in range(width):
            out_ref[c] = sums[n][:, c * size : (c + 1) * size].astype(out_ref.dtype)


def own_kernel(
    blocks, own, lines, voxel_ref, line_ref, rows_ref, image_ref, tiles_ref, counts_ref,
    background_ref, activity_ref, sensitivity_ref, base_ref, measured_ref, ratio_ref, matrix_ref,
    gain_ref, slot_ref, order_ref,
):
    size = tiles_ref.shape[-1]
    width = (lines - own) // 2
    index_tiles(voxel_ref, line_ref, slot_ref, blocks, lines)
    for j in range(width):
        order_ref[j] = rows_ref[j]
    at = jnp.int32(width)
    for o in range(own):
        oblique = functools.reduce(jnp.logical_or, [rows_ref[j] == o for j in range(width)])
        order_ref[jnp.where(oblique, own, at)] = o
        at = at + jnp.where(oblique, 0, 1)
    image = image_ref[...]
    for start in range(0, own, width):
        which = [order_ref[start + c] for c in range(width)]
        sums = project(image, tiles_ref, slot_ref, range(blocks), which, lines)
        for c, row in enumerate(which):
            base = sums[:, c * size : (c + 1) * size].T + background_ref[row].astype(jnp.float32)
            measured = counts_ref[row].astype(jnp.float32)
            if start == 0:
                base_ref[c] = base
                measured_ref[c] = measured
            else:
                ratio_ref[start - width + c] = (measured / base).astype(ratio_ref.dtype)
    away = (1 - home_half()) * (blocks // 2)
    for v in range(blocks):
        voxel = lax.rem(away + v, blocks)
        for c in range(lines):
            line = order_ref[c] if c < own else c
            matrix_ref[v * size : (v + 1) * size, c * size : (c + 1) * size] = tile_of(
                tiles_ref, slot_ref, voxel, line, lines
            )
    fill_gain(size, activity_ref, sensitivity_ref, gain_ref)


def oblique_kernel(slabs, forth_ref, back_ref, base_ref, measured_ref, out_ref):
    _, has_forth, has_back = place(slabs)
    for j in range(out_ref.shape[0]):
        forth = forth_ref[j].astype(jnp.float32)
        back = back_ref[j].astype(jnp.float32)
        extra = jnp.where(has_forth, forth, 0.0) + jnp.where(has_back, back, 0.0)
        out_ref[j] = (measured_ref[j] / (base_ref[j] + extra.T)).astype(out_ref.dtype)


def own_back_kernel(own, matrix_ref, oblique_ref, ratio_ref, out_ref):
    size = ratio_ref.shape[1]
    ratios = jnp.concatenate([oblique_ref[...], ratio_ref[...]], axis=0)
    ratios = ratios.reshape(own * size, -1)
    out_ref[...] = jnp.dot(
        matrix_ref[:, : own * size], ratios, preferred_element_type=jnp.float32
    )


def fill_gain(size, activity_ref, sensitivity_ref, gain_ref):
    count = gain_ref.shape[0] // size
    first = home_half() * count
    for n in range(count):
        at = pl.multiple_of((first + n) * size, size)
        values = activity_ref[pl.ds(at, size)].astype(jnp.float32)
        sens = sensitivity_ref[pl.ds(first + n, 1)]
        gain = values / jnp.broadcast_to(sens, (size, size)).T
        gain_ref[n * size : (n + 1) * size] = gain * (1.0 / CHIP_SCALE)


def edge_back_kernel(slabs, own, start, scale, matrix_ref, back_ref, forth_ref, own_ref, out_ref):
    size = forth_ref.shape[1]
    rows = out_ref.shape[0]
    odd, has_forth, has_back = place(slabs)
    forth = jnp.where(has_forth, forth_ref[...], jnp.zeros_like(forth_ref))
    back = jnp.where(has_back, back_ref[...], jnp.zeros_like(back_ref))
    left = jnp.where(odd == 0, back, forth)
    right = jnp.where(odd == 0, forth, back)
    ratios = jnp.concatenate([left, right], axis=0)
    ratios = ratios.reshape(ratios.shape[0] * size, -1)
    sums = jnp.dot(
        matrix_ref[start : start + rows, own * size :], ratios, preferred_element_type=jnp.float32
    )
    out_ref[...] = (sums + own_ref[start : start + rows]) * scale


def write_rows_kernel(half_rows, places, *refs):
    out_hbm, sem = refs[-2:]
    odd = home_half()
    copies = []
    for n, (turn, start) in enumerate(places):
        count = refs[n].shape[0]
        at = pl.multiple_of((odd + turn) % 2 * half_rows + start, 32)
        copies.append(
            pltpu.make_async_copy(refs[n], out_hbm.at[pl.ds(at, count)], sem.at[n])
        )
    for copy in copies:
        copy.start()
    for copy in copies:
        copy.wait()


def body(
    slabs, angles, activity, sensitivity, system_tiles, tile_voxel, tile_line, oblique_rows,
    counts, background,
):
    size = system_tiles.shape[-1]
    frames = activity.shape[1]
    blocks = activity.shape[0] // size
    own = counts.shape[2] // size
    width = oblique_rows.shape[-1]
    lines = own + 2 * width
    half = blocks // 2
    tiles = system_tiles[0, 0]
    voxel = tile_voxel[0, 0]
    line = tile_line[0, 0]
    rows = oblique_rows[0, 0]
    measured = counts[0, 0].reshape(own, size, frames)
    additive = background[0, 0].reshape(own, size, frames)

    forth = []
    for s in range(slabs):
        for a in range(angles):
            t = s - 1 if a % 2 == 0 else s + 1
            here = s * angles + a
            there = t * angles + a if 0 <= t < slabs else s * angles + (a ^ 1)
            forth.append((here, there))
    back = [(there, here) for here, there in forth]
    both = ("slab", "angle")
    slots = pltpu.SMEM((blocks * (lines + 1),), jnp.int32)

    def array(dtype, *shape):
        return jax.ShapeDtypeStruct(shape, dtype)

    edge_forth, edge_back, image, held = pl.pallas_call(
        functools.partial(edge_kernel, blocks, own, lines),
        out_shape=(
            array(jnp.bfloat16, width, frames, size),
            array(jnp.bfloat16, width, frames, size),
            array(jnp.bfloat16, frames, blocks * size),
            array(jnp.bfloat16, *tiles.shape),
        ),
        in_specs=[HBM] * 4,
        out_specs=(VMEM,) * 4,
        scratch_shapes=[
            pltpu.SMEM(voxel.shape, jnp.int32),
            pltpu.SMEM(line.shape, jnp.int32),
            pltpu.VMEM(activity.shape, activity.dtype),
            slots,
            pltpu.SemaphoreType.DMA((3,)),
            pltpu.SemaphoreType.DMA((pl.cdiv(tiles.shape[0], PIECE),)),
        ],
        compiler_params=params(),
        name="edge_partials",
    )(*[pltpu.with_memory_space_constraint(a, pltpu.HBM) for a in (voxel, line, activity, tiles)])
    got_forth = lax.ppermute(edge_forth, both, forth)
    got_back = lax.ppermute(edge_back, both, back)
    half_rows = half * size
    base, taken, ratio, matrix, gain = pl.pallas_call(
        functools.partial(own_kernel, blocks, own, lines),
        out_shape=(
            array(jnp.float32, width, size, frames),
            array(jnp.float32, width, size, frames),
            array(jnp.bfloat16, own - width, size, frames),
            array(jnp.bfloat16, blocks * size, lines * size),
            array(jnp.float32, half_rows, frames),
        ),
        in_specs=[SMEM] * 3 + [VMEM] * 6,
        out_specs=(VMEM,) * 5,
        scratch_shapes=[slots, pltpu.SMEM((own + 1,), jnp.int32)],
        compiler_params=params(),
        name="own_partials",
    )(
        voxel, line, rows, image, held, measured, additive, activity,
        sensitivity.reshape(blocks, size),
    )
    oblique = pl.pallas_call(
        functools.partial(oblique_kernel, slabs),
        out_shape=array(jnp.bfloat16, width, size, frames),
        in_specs=[VMEM] * 4,
        out_specs=VMEM,
        compiler_params=params(),
        name="oblique_ratios",
    )(got_forth, got_back, base, taken)
    beside_forth = lax.ppermute(oblique, both, forth)
    beside_back = lax.ppermute(oblique, both, back)
    own_back = pl.pallas_call(
        functools.partial(own_back_kernel, own),
        out_shape=array(jnp.float32, blocks * size, frames),
        in_specs=[VMEM] * 3,
        out_specs=VMEM,
        compiler_params=params(),
        name="own_back",
    )(matrix, oblique, ratio)

    def edge_rows(start, count, scale, name, after=None):
        return pl.pallas_call(
            functools.partial(edge_back_kernel, slabs, own, start, scale),
            out_shape=array(jnp.float32, count, frames),
            in_specs=[VMEM] * 4,
            out_specs=VMEM,
            compiler_params=params(),
            name=name,
        )(matrix, beside_back if after is None else after, beside_forth, own_back)

    def wide(values):
        return values.astype(jnp.float32)

    def write_rows(image_now, name, *parts):
        values = [part[0] for part in parts]
        places = [part[1:] for part in parts]
        before = [] if image_now is None else [image_now]
        return pl.pallas_call(
            functools.partial(write_rows_kernel, half_rows, places),
            out_shape=array(jnp.bfloat16, blocks * size, frames),
            in_specs=[VMEM] * len(values) + [HBM] * len(before),
            out_specs=HBM,
            scratch_shapes=[pltpu.SemaphoreType.DMA((len(values),))],
            input_output_aliases={len(values): 0} if before else {},
            compiler_params=params(),
            name=name,
        )(*values, *before)

    pairs = [(a, a ^ 1) for a in range(angles)]
    cuts = [0, FIRST_PART * half_rows // 24, half_rows]
    cuts = [0, FIRST_PART * half_rows // 24, half_rows]
    spans = [slice(at, end) for at, end in zip(cuts[:-1], cuts[1:])]
    got = []
    for n, span in enumerate(spans):
        away = edge_rows(span.start, span.stop - span.start, PART_SCALE, f"edge_back_sent_{n}")
        got.append(lax.ppermute(away.astype(jnp.float16), "angle", pairs))
    written = []
    for n, (at, end) in enumerate(zip(cuts[:-1], cuts[1:])):
        span = spans[n]
        after, got[n] = lax.optimization_barrier((beside_back, got[n])) if n else (None, got[n])
        home = edge_rows(half_rows + at, end - at, 1.0, f"edge_back_kept_{n}", after)
        chip = (home + wide(got[n]) * (1.0 / PART_SCALE)) * CHIP_SCALE
        if angles == 4:
            chip = lax.optimization_barrier(chip.astype(jnp.float16))
            across = lax.ppermute(chip, "angle", [(a, a ^ 3) for a in range(angles)])
            if written:
                across, rows_away = lax.optimization_barrier((across, rows_away))
                written[-1] = (rows_away,) + written[-1][1:]
            total = wide(chip) + wide(across)
        else:
            groups = [[a for a in range(angles) if (a + a // 2) % 2 == n] for n in range(2)]
            total = lax.psum(chip, "angle", axis_index_groups=groups)
        rows_home = (gain[span] * total).astype(jnp.bfloat16)
        rows_home = lax.optimization_barrier(rows_home)
        rows_away = lax.ppermute(rows_home, "angle", pairs)
        written += [(rows_home, 0, at), (rows_away, 1, at)]
    updated = write_rows(None, "write_first", *written[:-1])
    return write_rows(updated, "write_last", written[-1])


def solution(mesh):
    placed = (
        P(("groups", "slab"), None),
        P(("groups", "slab")),
        P(("groups", "slab"), "angle", None, None, None),
        P(("groups", "slab"), "angle", None),
        P(("groups", "slab"), "angle", None),
        P(("groups", "slab"), "angle", None),
        P(("groups", "slab"), "angle", None, None),
        P(("groups", "slab"), "angle", None, None),
    )
    return jax.shard_map(
        functools.partial(body, mesh.shape["slab"], mesh.shape["angle"]),
        mesh=mesh,
        in_specs=placed,
        out_specs=P(("groups", "slab"), None),
        check_vma=False,
    )
```

```python
import functools

import jax
import jax.numpy as jnp
from jax import lax
from jax.experimental import pallas as pl
from jax.experimental.pallas import tpu as pltpu
from jax.sharding import PartitionSpec as P

VMEM = pl.BlockSpec(memory_space=pltpu.VMEM)
SMEM = pl.BlockSpec(memory_space=pltpu.SMEM)
HBM = pl.BlockSpec(memory_space=pltpu.HBM)
PART_SCALE = 256.0
CHIP_SCALE = 128.0
GROUP = 2
PIECE = 16
FIRST_PART = 11


def params(mebibytes=16):
    return pltpu.CompilerParams(vmem_limit_bytes=mebibytes * 1024 * 1024)


def place(slabs):
    slab = lax.axis_index("slab")
    odd = lax.axis_index("angle") % 2
    left = slab > 0
    right = slab < slabs - 1
    even = odd == 0
    forth = jnp.logical_or(jnp.logical_and(even, right), jnp.logical_and(~even, left))
    back = jnp.logical_or(jnp.logical_and(even, left), jnp.logical_and(~even, right))
    return odd, forth, back


def home_half():
    angle = lax.axis_index("angle")
    return (angle + angle // 2) % 2


def index_tiles(voxel_ref, line_ref, slot_ref, blocks, lines):
    stride = lines + 1
    for n in range(blocks * stride):
        slot_ref[n] = -1
    for k in range(voxel_ref.shape[-1]):
        slot_ref[voxel_ref[k] * stride + line_ref[k]] = k


def tile_of(tiles_ref, slot_ref, voxel, line, lines):
    slot = slot_ref[voxel * (lines + 1) + line]
    tile = tiles_ref[jnp.maximum(slot, 0)]
    return jnp.where(slot >= 0, tile, jnp.zeros_like(tile))


def project(image, tiles_ref, slot_ref, voxels, which, lines):
    weights = jnp.concatenate(
        [
            jnp.concatenate([tile_of(tiles_ref, slot_ref, v, c, lines) for c in which], axis=1)
            for v in voxels
        ],
        axis=0,
    )
    return jnp.dot(image, weights, preferred_element_type=jnp.float32)


def edge_kernel(
    blocks, own, lines, voxel_hbm, line_hbm, activity_hbm, tiles_hbm,
    forth_ref, back_ref, image_ref, tiles_ref,
    voxel_ref, line_ref, activity_ref, slot_ref, small_sem, tile_sem,
):
    size = tiles_ref.shape[-1]
    total = tiles_ref.shape[0]
    width = (lines - own) // 2
    first = [
        pltpu.make_async_copy(voxel_hbm, voxel_ref, small_sem.at[0]),
        pltpu.make_async_copy(line_hbm, line_ref, small_sem.at[1]),
        pltpu.make_async_copy(activity_hbm, activity_ref, small_sem.at[2]),
    ]
    pieces = []
    for n, start in enumerate(range(0, total, PIECE)):
        span = pl.ds(start, min(PIECE, total - start))
        pieces.append(
            pltpu.make_async_copy(tiles_hbm.at[span], tiles_ref.at[span], tile_sem.at[n])
        )
    for copy in first:
        copy.start()
    for copy in pieces:
        copy.start(priority=1)
    first[0].wait()
    first[1].wait()
    index_tiles(voxel_ref, line_ref, slot_ref, blocks, lines)
    first[2].wait()
    for v in range(blocks):
        image_ref[:, v * size : (v + 1) * size] = activity_ref[v * size : (v + 1) * size, :].T
    odd = lax.axis_index("angle") % 2
    outs = (
        (forth_ref, own + width * odd),
        (back_ref, own + width * (1 - odd)),
    )
    sums = [None, None]
    waited = 0
    for low in range(0, blocks, GROUP):
        high = min(low + GROUP, blocks)
        needed = len(pieces) if high == blocks else min(len(pieces), pl.cdiv(high * lines, PIECE))
        for copy in pieces[waited:needed]:
            copy.wait()
        waited = needed
        image = image_ref[:, low * size : high * size]
        for n, (_, start) in enumerate(outs):
            which = [start + c for c in range(width)]
            part = project(image, tiles_ref, slot_ref, range(low, high), which, lines)
            sums[n] = part if sums[n] is None else sums[n] + part
    for n, (out_ref, _) in enumerate(outs):
        for c in range(width):
            out_ref[c] = sums[n][:, c * size : (c + 1) * size].astype(out_ref.dtype)


def own_kernel(
    blocks, own, lines, voxel_ref, line_ref, rows_ref, image_ref, tiles_ref, counts_ref,
    background_ref, activity_ref, sensitivity_ref, base_ref, measured_ref, ratio_ref, matrix_ref,
    gain_ref, slot_ref, order_ref,
):
    size = tiles_ref.shape[-1]
    width = (lines - own) // 2
    index_tiles(voxel_ref, line_ref, slot_ref, blocks, lines)
    for j in range(width):
        order_ref[j] = rows_ref[j]
    at = jnp.int32(width)
    for o in range(own):
        oblique = functools.reduce(jnp.logical_or, [rows_ref[j] == o for j in range(width)])
        order_ref[jnp.where(oblique, own, at)] = o
        at = at + jnp.where(oblique, 0, 1)
    image = image_ref[...]
    for start in range(0, own, width):
        which = [order_ref[start + c] for c in range(width)]
        sums = project(image, tiles_ref, slot_ref, range(blocks), which, lines)
        for c, row in enumerate(which):
            base = sums[:, c * size : (c + 1) * size].T + background_ref[row].astype(jnp.float32)
            measured = counts_ref[row].astype(jnp.float32)
            if start == 0:
                base_ref[c] = base
                measured_ref[c] = measured
            else:
                ratio_ref[start - width + c] = (measured / base).astype(ratio_ref.dtype)
    away = (1 - home_half()) * (blocks // 2)
    for v in range(blocks):
        voxel = lax.rem(away + v, blocks)
        for c in range(lines):
            line = order_ref[c] if c < own else c
            matrix_ref[v * size : (v + 1) * size, c * size : (c + 1) * size] = tile_of(
                tiles_ref, slot_ref, voxel, line, lines
            )
    fill_gain(size, activity_ref, sensitivity_ref, gain_ref)


def oblique_kernel(slabs, forth_ref, back_ref, base_ref, measured_ref, out_ref):
    _, has_forth, has_back = place(slabs)
    for j in range(out_ref.shape[0]):
        forth = forth_ref[j].astype(jnp.float32)
        back = back_ref[j].astype(jnp.float32)
        extra = jnp.where(has_forth, forth, 0.0) + jnp.where(has_back, back, 0.0)
        out_ref[j] = (measured_ref[j] / (base_ref[j] + extra.T)).astype(out_ref.dtype)


def own_back_kernel(own, matrix_ref, oblique_ref, ratio_ref, out_ref):
    size = ratio_ref.shape[1]
    ratios = jnp.concatenate([oblique_ref[...], ratio_ref[...]], axis=0)
    ratios = ratios.reshape(own * size, -1)
    out_ref[...] = jnp.dot(
        matrix_ref[:, : own * size], ratios, preferred_element_type=jnp.float32
    )


def fill_gain(size, activity_ref, sensitivity_ref, gain_ref):
    count = gain_ref.shape[0] // size
    first = home_half() * count
    for n in range(count):
        at = pl.multiple_of((first + n) * size, size)
        values = activity_ref[pl.ds(at, size)].astype(jnp.float32)
        sens = sensitivity_ref[pl.ds(first + n, 1)]
        gain = values / jnp.broadcast_to(sens, (size, size)).T
        gain_ref[n * size : (n + 1) * size] = gain * (1.0 / CHIP_SCALE)


def edge_back_kernel(slabs, own, start, scale, matrix_ref, back_ref, forth_ref, own_ref, out_ref):
    size = forth_ref.shape[1]
    rows = out_ref.shape[0]
    odd, has_forth, has_back = place(slabs)
    forth = jnp.where(has_forth, forth_ref[...], jnp.zeros_like(forth_ref))
    back = jnp.where(has_back, back_ref[...], jnp.zeros_like(back_ref))
    left = jnp.where(odd == 0, back, forth)
    right = jnp.where(odd == 0, forth, back)
    ratios = jnp.concatenate([left, right], axis=0)
    ratios = ratios.reshape(ratios.shape[0] * size, -1)
    sums = jnp.dot(
        matrix_ref[start : start + rows, own * size :], ratios, preferred_element_type=jnp.float32
    )
    out_ref[...] = (sums + own_ref[start : start + rows]) * scale


def write_rows_kernel(half_rows, places, *refs):
    out_hbm, sem = refs[-2:]
    odd = home_half()
    copies = []
    for n, (turn, start) in enumerate(places):
        count = refs[n].shape[0]
        at = pl.multiple_of((odd + turn) % 2 * half_rows + start, 32)
        copies.append(
            pltpu.make_async_copy(refs[n], out_hbm.at[pl.ds(at, count)], sem.at[n])
        )
    for copy in copies:
        copy.start()
    for copy in copies:
        copy.wait()


def body(
    slabs, angles, activity, sensitivity, system_tiles, tile_voxel, tile_line, oblique_rows,
    counts, background,
):
    size = system_tiles.shape[-1]
    frames = activity.shape[1]
    blocks = activity.shape[0] // size
    own = counts.shape[2] // size
    width = oblique_rows.shape[-1]
    lines = own + 2 * width
    half = blocks // 2
    tiles = system_tiles[0, 0]
    voxel = tile_voxel[0, 0]
    line = tile_line[0, 0]
    rows = oblique_rows[0, 0]
    measured = counts[0, 0].reshape(own, size, frames)
    additive = background[0, 0].reshape(own, size, frames)

    forth = []
    for s in range(slabs):
        for a in range(angles):
            t = s - 1 if a % 2 == 0 else s + 1
            here = s * angles + a
            there = t * angles + a if 0 <= t < slabs else s * angles + (a ^ 1)
            forth.append((here, there))
    back = [(there, here) for here, there in forth]
    both = ("slab", "angle")
    slots = pltpu.SMEM((blocks * (lines + 1),), jnp.int32)

    def array(dtype, *shape):
        return jax.ShapeDtypeStruct(shape, dtype)

    edge_forth, edge_back, image, held = pl.pallas_call(
        functools.partial(edge_kernel, blocks, own, lines),
        out_shape=(
            array(jnp.bfloat16, width, frames, size),
            array(jnp.bfloat16, width, frames, size),
            array(jnp.bfloat16, frames, blocks * size),
            array(jnp.bfloat16, *tiles.shape),
        ),
        in_specs=[HBM] * 4,
        out_specs=(VMEM,) * 4,
        scratch_shapes=[
            pltpu.SMEM(voxel.shape, jnp.int32),
            pltpu.SMEM(line.shape, jnp.int32),
            pltpu.VMEM(activity.shape, activity.dtype),
            slots,
            pltpu.SemaphoreType.DMA((3,)),
            pltpu.SemaphoreType.DMA((pl.cdiv(tiles.shape[0], PIECE),)),
        ],
        compiler_params=params(),
        name="edge_partials",
    )(*[pltpu.with_memory_space_constraint(a, pltpu.HBM) for a in (voxel, line, activity, tiles)])
    got_forth = lax.ppermute(edge_forth, both, forth)
    got_back = lax.ppermute(edge_back, both, back)
    half_rows = half * size
    base, taken, ratio, matrix, gain = pl.pallas_call(
        functools.partial(own_kernel, blocks, own, lines),
        out_shape=(
            array(jnp.float32, width, size, frames),
            array(jnp.float32, width, size, frames),
            array(jnp.bfloat16, own - width, size, frames),
            array(jnp.bfloat16, blocks * size, lines * size),
            array(jnp.float32, half_rows, frames),
        ),
        in_specs=[SMEM] * 3 + [VMEM] * 6,
        out_specs=(VMEM,) * 5,
        scratch_shapes=[slots, pltpu.SMEM((own + 1,), jnp.int32)],
        compiler_params=params(),
        name="own_partials",
    )(
        voxel, line, rows, image, held, measured, additive, activity,
        sensitivity.reshape(blocks, size),
    )
    oblique = pl.pallas_call(
        functools.partial(oblique_kernel, slabs),
        out_shape=array(jnp.bfloat16, width, size, frames),
        in_specs=[VMEM] * 4,
        out_specs=VMEM,
        compiler_params=params(),
        name="oblique_ratios",
    )(got_forth, got_back, base, taken)
    beside_forth = lax.ppermute(oblique, both, forth)
    beside_back = lax.ppermute(oblique, both, back)
    own_back = pl.pallas_call(
        functools.partial(own_back_kernel, own),
        out_shape=array(jnp.float32, blocks * size, frames),
        in_specs=[VMEM] * 3,
        out_specs=VMEM,
        compiler_params=params(),
        name="own_back",
    )(matrix, oblique, ratio)

    def edge_rows(start, count, scale, name):
        return pl.pallas_call(
            functools.partial(edge_back_kernel, slabs, own, start, scale),
            out_shape=array(jnp.float32, count, frames),
            in_specs=[VMEM] * 4,
            out_specs=VMEM,
            compiler_params=params(),
            name=name,
        )(matrix, beside_back, beside_forth, own_back)

    def wide(values):
        return values.astype(jnp.float32)

    def write_rows(image_now, name, *parts):
        values = [part[0] for part in parts]
        places = [part[1:] for part in parts]
        before = [] if image_now is None else [image_now]
        return pl.pallas_call(
            functools.partial(write_rows_kernel, half_rows, places),
            out_shape=array(jnp.bfloat16, blocks * size, frames),
            in_specs=[VMEM] * len(values) + [HBM] * len(before),
            out_specs=HBM,
            scratch_shapes=[pltpu.SemaphoreType.DMA((len(values),))],
            input_output_aliases={len(values): 0} if before else {},
            compiler_params=params(),
            name=name,
        )(*values, *before)

    pairs = [(a, a ^ 1) for a in range(angles)]
    cuts = [0, FIRST_PART * half_rows // 24, half_rows]
    cuts = [0, FIRST_PART * half_rows // 24, half_rows]
    spans = [slice(at, end) for at, end in zip(cuts[:-1], cuts[1:])]
    got = []
    for n, span in enumerate(spans):
        away = edge_rows(span.start, span.stop - span.start, PART_SCALE, f"edge_back_sent_{n}")
        got.append(lax.ppermute(away.astype(jnp.float16), "angle", pairs))
    home = edge_rows(half_rows, half_rows, 1.0, "edge_back_kept")
    written = []
    for n, (at, end) in enumerate(zip(cuts[:-1], cuts[1:])):
        span = spans[n]
        chip = (home[span] + wide(got[n]) * (1.0 / PART_SCALE)) * CHIP_SCALE
        if angles == 4:
            chip = lax.optimization_barrier(chip.astype(jnp.float16))
            across = lax.ppermute(chip, "angle", [(a, a ^ 3) for a in range(angles)])
            if written:
                across, rows_away = lax.optimization_barrier((across, rows_away))
                written[-1] = (rows_away,) + written[-1][1:]
            total = wide(chip) + wide(across)
        else:
            groups = [[a for a in range(angles) if (a + a // 2) % 2 == n] for n in range(2)]
            total = lax.psum(chip, "angle", axis_index_groups=groups)
        rows_home = (gain[span] * total).astype(jnp.bfloat16)
        rows_home = lax.optimization_barrier(rows_home)
        rows_away = lax.ppermute(rows_home, "angle", pairs)
        written += [(rows_home, 0, at), (rows_away, 1, at)]
    updated = write_rows(None, "write_first", *written[:-1])
    return write_rows(updated, "write_last", written[-1])


def solution(mesh):
    placed = (
        P(("groups", "slab"), None),
        P(("groups", "slab")),
        P(("groups", "slab"), "angle", None, None, None),
        P(("groups", "slab"), "angle", None),
        P(("groups", "slab"), "angle", None),
        P(("groups", "slab"), "angle", None),
        P(("groups", "slab"), "angle", None, None),
        P(("groups", "slab"), "angle", None, None),
    )
    return jax.shard_map(
        functools.partial(body, mesh.shape["slab"], mesh.shape["angle"]),
        mesh=mesh,
        in_specs=placed,
        out_specs=P(("groups", "slab"), None),
        check_vma=False,
    )
```

```python
import functools

import jax
import jax.numpy as jnp
from jax import lax
from jax.experimental import pallas as pl
from jax.experimental.pallas import tpu as pltpu
from jax.sharding import PartitionSpec as P

VMEM = pl.BlockSpec(memory_space=pltpu.VMEM)
SMEM = pl.BlockSpec(memory_space=pltpu.SMEM)
HBM = pl.BlockSpec(memory_space=pltpu.HBM)
PART_SCALE = 256.0
CHIP_SCALE = 128.0
GROUP = 2
PIECE = 16
FIRST_PART = 7


def params(mebibytes=16):
    return pltpu.CompilerParams(vmem_limit_bytes=mebibytes * 1024 * 1024)


def place(slabs):
    slab = lax.axis_index("slab")
    odd = lax.axis_index("angle") % 2
    left = slab > 0
    right = slab < slabs - 1
    even = odd == 0
    forth = jnp.logical_or(jnp.logical_and(even, right), jnp.logical_and(~even, left))
    back = jnp.logical_or(jnp.logical_and(even, left), jnp.logical_and(~even, right))
    return odd, forth, back


def home_half():
    angle = lax.axis_index("angle")
    return (angle + angle // 2) % 2


def index_tiles(voxel_ref, line_ref, slot_ref, blocks, lines):
    stride = lines + 1
    for n in range(blocks * stride):
        slot_ref[n] = -1
    for k in range(voxel_ref.shape[-1]):
        slot_ref[voxel_ref[k] * stride + line_ref[k]] = k


def tile_of(tiles_ref, slot_ref, voxel, line, lines):
    slot = slot_ref[voxel * (lines + 1) + line]
    tile = tiles_ref[jnp.maximum(slot, 0)]
    return jnp.where(slot >= 0, tile, jnp.zeros_like(tile))


def project(image, tiles_ref, slot_ref, voxels, which, lines):
    weights = jnp.concatenate(
        [
            jnp.concatenate([tile_of(tiles_ref, slot_ref, v, c, lines) for c in which], axis=1)
            for v in voxels
        ],
        axis=0,
    )
    return jnp.dot(image, weights, preferred_element_type=jnp.float32)


def edge_kernel(
    blocks, own, lines, voxel_hbm, line_hbm, activity_hbm, tiles_hbm,
    forth_ref, back_ref, image_ref, tiles_ref,
    voxel_ref, line_ref, activity_ref, slot_ref, small_sem, tile_sem,
):
    size = tiles_ref.shape[-1]
    total = tiles_ref.shape[0]
    width = (lines - own) // 2
    first = [
        pltpu.make_async_copy(voxel_hbm, voxel_ref, small_sem.at[0]),
        pltpu.make_async_copy(line_hbm, line_ref, small_sem.at[1]),
        pltpu.make_async_copy(activity_hbm, activity_ref, small_sem.at[2]),
    ]
    pieces = []
    for n, start in enumerate(range(0, total, PIECE)):
        span = pl.ds(start, min(PIECE, total - start))
        pieces.append(
            pltpu.make_async_copy(tiles_hbm.at[span], tiles_ref.at[span], tile_sem.at[n])
        )
    for copy in first:
        copy.start()
    for copy in pieces:
        copy.start(priority=1)
    first[0].wait()
    first[1].wait()
    index_tiles(voxel_ref, line_ref, slot_ref, blocks, lines)
    first[2].wait()
    for v in range(blocks):
        image_ref[:, v * size : (v + 1) * size] = activity_ref[v * size : (v + 1) * size, :].T
    odd = lax.axis_index("angle") % 2
    outs = (
        (forth_ref, own + width * odd),
        (back_ref, own + width * (1 - odd)),
    )
    sums = [None, None]
    waited = 0
    for low in range(0, blocks, GROUP):
        high = min(low + GROUP, blocks)
        needed = len(pieces) if high == blocks else min(len(pieces), pl.cdiv(high * lines, PIECE))
        for copy in pieces[waited:needed]:
            copy.wait()
        waited = needed
        image = image_ref[:, low * size : high * size]
        for n, (_, start) in enumerate(outs):
            which = [start + c for c in range(width)]
            part = project(image, tiles_ref, slot_ref, range(low, high), which, lines)
            sums[n] = part if sums[n] is None else sums[n] + part
    for n, (out_ref, _) in enumerate(outs):
        for c in range(width):
            out_ref[c] = sums[n][:, c * size : (c + 1) * size].astype(out_ref.dtype)


def own_kernel(
    blocks, own, lines, voxel_ref, line_ref, rows_ref, image_ref, tiles_ref, counts_ref,
    background_ref, activity_ref, sensitivity_ref, base_ref, measured_ref, ratio_ref, matrix_ref,
    gain_ref, slot_ref, order_ref,
):
    size = tiles_ref.shape[-1]
    width = (lines - own) // 2
    index_tiles(voxel_ref, line_ref, slot_ref, blocks, lines)
    for j in range(width):
        order_ref[j] = rows_ref[j]
    at = jnp.int32(width)
    for o in range(own):
        oblique = functools.reduce(jnp.logical_or, [rows_ref[j] == o for j in range(width)])
        order_ref[jnp.where(oblique, own, at)] = o
        at = at + jnp.where(oblique, 0, 1)
    image = image_ref[...]
    for start in range(0, own, width):
        which = [order_ref[start + c] for c in range(width)]
        sums = project(image, tiles_ref, slot_ref, range(blocks), which, lines)
        for c, row in enumerate(which):
            base = sums[:, c * size : (c + 1) * size].T + background_ref[row].astype(jnp.float32)
            measured = counts_ref[row].astype(jnp.float32)
            if start == 0:
                base_ref[c] = base
                measured_ref[c] = measured
            else:
                ratio_ref[start - width + c] = (measured / base).astype(ratio_ref.dtype)
    away = (1 - home_half()) * (blocks // 2)
    for v in range(blocks):
        voxel = lax.rem(away + v, blocks)
        for c in range(lines):
            line = order_ref[c] if c < own else c
            matrix_ref[v * size : (v + 1) * size, c * size : (c + 1) * size] = tile_of(
                tiles_ref, slot_ref, voxel, line, lines
            )
    fill_gain(size, activity_ref, sensitivity_ref, gain_ref)


def oblique_kernel(slabs, forth_ref, back_ref, base_ref, measured_ref, out_ref):
    _, has_forth, has_back = place(slabs)
    for j in range(out_ref.shape[0]):
        forth = forth_ref[j].astype(jnp.float32)
        back = back_ref[j].astype(jnp.float32)
        extra = jnp.where(has_forth, forth, 0.0) + jnp.where(has_back, back, 0.0)
        out_ref[j] = (measured_ref[j] / (base_ref[j] + extra.T)).astype(out_ref.dtype)


def own_back_kernel(own, matrix_ref, oblique_ref, ratio_ref, out_ref):
    size = ratio_ref.shape[1]
    ratios = jnp.concatenate([oblique_ref[...], ratio_ref[...]], axis=0)
    ratios = ratios.reshape(own * size, -1)
    out_ref[...] = jnp.dot(
        matrix_ref[:, : own * size], ratios, preferred_element_type=jnp.float32
    )


def fill_gain(size, activity_ref, sensitivity_ref, gain_ref):
    count = gain_ref.shape[0] // size
    first = home_half() * count
    for n in range(count):
        at = pl.multiple_of((first + n) * size, size)
        values = activity_ref[pl.ds(at, size)].astype(jnp.float32)
        sens = sensitivity_ref[pl.ds(first + n, 1)]
        gain = values / jnp.broadcast_to(sens, (size, size)).T
        gain_ref[n * size : (n + 1) * size] = gain * (1.0 / CHIP_SCALE)


def edge_back_kernel(slabs, own, start, scale, matrix_ref, back_ref, forth_ref, own_ref, out_ref):
    size = forth_ref.shape[1]
    rows = out_ref.shape[0]
    odd, has_forth, has_back = place(slabs)
    forth = jnp.where(has_forth, forth_ref[...], jnp.zeros_like(forth_ref))
    back = jnp.where(has_back, back_ref[...], jnp.zeros_like(back_ref))
    left = jnp.where(odd == 0, back, forth)
    right = jnp.where(odd == 0, forth, back)
    ratios = jnp.concatenate([left, right], axis=0)
    ratios = ratios.reshape(ratios.shape[0] * size, -1)
    sums = jnp.dot(
        matrix_ref[start : start + rows, own * size :], ratios, preferred_element_type=jnp.float32
    )
    out_ref[...] = (sums + own_ref[start : start + rows]) * scale


def write_rows_kernel(half_rows, places, *refs):
    out_hbm, sem = refs[-2:]
    odd = home_half()
    copies = []
    for n, (turn, start) in enumerate(places):
        count = refs[n].shape[0]
        at = pl.multiple_of((odd + turn) % 2 * half_rows + start, 16)
        copies.append(
            pltpu.make_async_copy(refs[n], out_hbm.at[pl.ds(at, count)], sem.at[n])
        )
    for copy in copies:
        copy.start()
    for copy in copies:
        copy.wait()


def body(
    slabs, angles, activity, sensitivity, system_tiles, tile_voxel, tile_line, oblique_rows,
    counts, background,
):
    size = system_tiles.shape[-1]
    frames = activity.shape[1]
    blocks = activity.shape[0] // size
    own = counts.shape[2] // size
    width = oblique_rows.shape[-1]
    lines = own + 2 * width
    half = blocks // 2
    tiles = system_tiles[0, 0]
    voxel = tile_voxel[0, 0]
    line = tile_line[0, 0]
    rows = oblique_rows[0, 0]
    measured = counts[0, 0].reshape(own, size, frames)
    additive = background[0, 0].reshape(own, size, frames)

    forth = []
    for s in range(slabs):
        for a in range(angles):
            t = s - 1 if a % 2 == 0 else s + 1
            here = s * angles + a
            there = t * angles + a if 0 <= t < slabs else s * angles + (a ^ 1)
            forth.append((here, there))
    back = [(there, here) for here, there in forth]
    both = ("slab", "angle")
    slots = pltpu.SMEM((blocks * (lines + 1),), jnp.int32)

    def array(dtype, *shape):
        return jax.ShapeDtypeStruct(shape, dtype)

    edge_forth, edge_back, image, held = pl.pallas_call(
        functools.partial(edge_kernel, blocks, own, lines),
        out_shape=(
            array(jnp.bfloat16, width, frames, size),
            array(jnp.bfloat16, width, frames, size),
            array(jnp.bfloat16, frames, blocks * size),
            array(jnp.bfloat16, *tiles.shape),
        ),
        in_specs=[HBM] * 4,
        out_specs=(VMEM,) * 4,
        scratch_shapes=[
            pltpu.SMEM(voxel.shape, jnp.int32),
            pltpu.SMEM(line.shape, jnp.int32),
            pltpu.VMEM(activity.shape, activity.dtype),
            slots,
            pltpu.SemaphoreType.DMA((3,)),
            pltpu.SemaphoreType.DMA((pl.cdiv(tiles.shape[0], PIECE),)),
        ],
        compiler_params=params(),
        name="edge_partials",
    )(*[pltpu.with_memory_space_constraint(a, pltpu.HBM) for a in (voxel, line, activity, tiles)])
    got_forth = lax.ppermute(edge_forth, both, forth)
    got_back = lax.ppermute(edge_back, both, back)
    half_rows = half * size
    base, taken, ratio, matrix, gain = pl.pallas_call(
        functools.partial(own_kernel, blocks, own, lines),
        out_shape=(
            array(jnp.float32, width, size, frames),
            array(jnp.float32, width, size, frames),
            array(jnp.bfloat16, own - width, size, frames),
            array(jnp.bfloat16, blocks * size, lines * size),
            array(jnp.float32, half_rows, frames),
        ),
        in_specs=[SMEM] * 3 + [VMEM] * 6,
        out_specs=(VMEM,) * 5,
        scratch_shapes=[slots, pltpu.SMEM((own + 1,), jnp.int32)],
        compiler_params=params(),
        name="own_partials",
    )(
        voxel, line, rows, image, held, measured, additive, activity,
        sensitivity.reshape(blocks, size),
    )
    oblique = pl.pallas_call(
        functools.partial(oblique_kernel, slabs),
        out_shape=array(jnp.bfloat16, width, size, frames),
        in_specs=[VMEM] * 4,
        out_specs=VMEM,
        compiler_params=params(),
        name="oblique_ratios",
    )(got_forth, got_back, base, taken)
    beside_forth = lax.ppermute(oblique, both, forth)
    beside_back = lax.ppermute(oblique, both, back)
    own_back = pl.pallas_call(
        functools.partial(own_back_kernel, own),
        out_shape=array(jnp.float32, blocks * size, frames),
        in_specs=[VMEM] * 3,
        out_specs=VMEM,
        compiler_params=params(),
        name="own_back",
    )(matrix, oblique, ratio)

    def edge_rows(start, count, scale, name):
        return pl.pallas_call(
            functools.partial(edge_back_kernel, slabs, own, start, scale),
            out_shape=array(jnp.float32, count, frames),
            in_specs=[VMEM] * 4,
            out_specs=VMEM,
            compiler_params=params(),
            name=name,
        )(matrix, beside_back, beside_forth, own_back)

    def wide(values):
        return values.astype(jnp.float32)

    def write_rows(image_now, name, *parts):
        values = [part[0] for part in parts]
        places = [part[1:] for part in parts]
        before = [] if image_now is None else [image_now]
        return pl.pallas_call(
            functools.partial(write_rows_kernel, half_rows, places),
            out_shape=array(jnp.bfloat16, blocks * size, frames),
            in_specs=[VMEM] * len(values) + [HBM] * len(before),
            out_specs=HBM,
            scratch_shapes=[pltpu.SemaphoreType.DMA((len(values),))],
            input_output_aliases={len(values): 0} if before else {},
            compiler_params=params(),
            name=name,
        )(*values, *before)

    pairs = [(a, a ^ 1) for a in range(angles)]
    cuts = [0, FIRST_PART * half_rows // 16, half_rows]
    spans = [slice(at, end) for at, end in zip(cuts[:-1], cuts[1:])]
    got = []
    for n, span in enumerate(spans):
        away = edge_rows(span.start, span.stop - span.start, PART_SCALE, f"edge_back_sent_{n}")
        got.append(lax.ppermute(away.astype(jnp.float16), "angle", pairs))
    home = edge_rows(half_rows, half_rows, 1.0, "edge_back_kept")
    written = []
    for n, (at, end) in enumerate(zip(cuts[:-1], cuts[1:])):
        span = spans[n]
        chip = (home[span] + wide(got[n]) * (1.0 / PART_SCALE)) * CHIP_SCALE
        if angles == 4:
            chip = lax.optimization_barrier(chip.astype(jnp.float16))
            across = lax.ppermute(chip, "angle", [(a, a ^ 3) for a in range(angles)])
            if written:
                across, rows_away = lax.optimization_barrier((across, rows_away))
                written[-1] = (rows_away,) + written[-1][1:]
            total = wide(chip) + wide(across)
        else:
            groups = [[a for a in range(angles) if (a + a // 2) % 2 == n] for n in range(2)]
            total = lax.psum(chip, "angle", axis_index_groups=groups)
        rows_home = (gain[span] * total).astype(jnp.bfloat16)
        rows_home = lax.optimization_barrier(rows_home)
        rows_away = lax.ppermute(rows_home, "angle", pairs)
        written += [(rows_home, 0, at), (rows_away, 1, at)]
    updated = write_rows(None, "write_first", *written[:-1])
    return write_rows(updated, "write_last", written[-1])


def solution(mesh):
    placed = (
        P(("groups", "slab"), None),
        P(("groups", "slab")),
        P(("groups", "slab"), "angle", None, None, None),
        P(("groups", "slab"), "angle", None),
        P(("groups", "slab"), "angle", None),
        P(("groups", "slab"), "angle", None),
        P(("groups", "slab"), "angle", None, None),
        P(("groups", "slab"), "angle", None, None),
    )
    return jax.shard_map(
        functools.partial(body, mesh.shape["slab"], mesh.shape["angle"]),
        mesh=mesh,
        in_specs=placed,
        out_specs=P(("groups", "slab"), None),
        check_vma=False,
    )
```

```python
import functools

import jax
import jax.numpy as jnp
from jax import lax
from jax.experimental import pallas as pl
from jax.experimental.pallas import tpu as pltpu
from jax.sharding import PartitionSpec as P

VMEM = pl.BlockSpec(memory_space=pltpu.VMEM)
SMEM = pl.BlockSpec(memory_space=pltpu.SMEM)
HBM = pl.BlockSpec(memory_space=pltpu.HBM)
PART_SCALE = 256.0
CHIP_SCALE = 128.0
GROUP = 2
PIECE = 16
FIRST_PART = 7


def params(mebibytes=16):
    return pltpu.CompilerParams(vmem_limit_bytes=mebibytes * 1024 * 1024)


def place(slabs):
    slab = lax.axis_index("slab")
    odd = lax.axis_index("angle") % 2
    left = slab > 0
    right = slab < slabs - 1
    even = odd == 0
    forth = jnp.logical_or(jnp.logical_and(even, right), jnp.logical_and(~even, left))
    back = jnp.logical_or(jnp.logical_and(even, left), jnp.logical_and(~even, right))
    return odd, forth, back


def home_half():
    angle = lax.axis_index("angle")
    return (angle + angle // 2) % 2


def index_tiles(voxel_ref, line_ref, slot_ref, blocks, lines):
    stride = lines + 1
    for n in range(blocks * stride):
        slot_ref[n] = -1
    for k in range(voxel_ref.shape[-1]):
        slot_ref[voxel_ref[k] * stride + line_ref[k]] = k


def tile_of(tiles_ref, slot_ref, voxel, line, lines):
    slot = slot_ref[voxel * (lines + 1) + line]
    tile = tiles_ref[jnp.maximum(slot, 0)]
    return jnp.where(slot >= 0, tile, jnp.zeros_like(tile))


def project(image, tiles_ref, slot_ref, voxels, which, lines):
    weights = jnp.concatenate(
        [
            jnp.concatenate([tile_of(tiles_ref, slot_ref, v, c, lines) for c in which], axis=1)
            for v in voxels
        ],
        axis=0,
    )
    return jnp.dot(image, weights, preferred_element_type=jnp.float32)


def edge_kernel(
    blocks, own, lines, voxel_hbm, line_hbm, activity_hbm, tiles_hbm,
    forth_ref, back_ref, image_ref, tiles_ref,
    voxel_ref, line_ref, activity_ref, slot_ref, small_sem, tile_sem,
):
    size = tiles_ref.shape[-1]
    total = tiles_ref.shape[0]
    width = (lines - own) // 2
    first = [
        pltpu.make_async_copy(voxel_hbm, voxel_ref, small_sem.at[0]),
        pltpu.make_async_copy(line_hbm, line_ref, small_sem.at[1]),
        pltpu.make_async_copy(activity_hbm, activity_ref, small_sem.at[2]),
    ]
    pieces = []
    for n, start in enumerate(range(0, total, PIECE)):
        span = pl.ds(start, min(PIECE, total - start))
        pieces.append(
            pltpu.make_async_copy(tiles_hbm.at[span], tiles_ref.at[span], tile_sem.at[n])
        )
    for copy in first:
        copy.start()
    for copy in pieces:
        copy.start(priority=1)
    first[0].wait()
    first[1].wait()
    index_tiles(voxel_ref, line_ref, slot_ref, blocks, lines)
    first[2].wait()
    for v in range(blocks):
        image_ref[:, v * size : (v + 1) * size] = activity_ref[v * size : (v + 1) * size, :].T
    odd = lax.axis_index("angle") % 2
    outs = (
        (forth_ref, own + width * odd),
        (back_ref, own + width * (1 - odd)),
    )
    sums = [None, None]
    waited = 0
    for low in range(0, blocks, GROUP):
        high = min(low + GROUP, blocks)
        needed = len(pieces) if high == blocks else min(len(pieces), pl.cdiv(high * lines, PIECE))
        for copy in pieces[waited:needed]:
            copy.wait()
        waited = needed
        image = image_ref[:, low * size : high * size]
        for n, (_, start) in enumerate(outs):
            which = [start + c for c in range(width)]
            part = project(image, tiles_ref, slot_ref, range(low, high), which, lines)
            sums[n] = part if sums[n] is None else sums[n] + part
    for n, (out_ref, _) in enumerate(outs):
        for c in range(width):
            out_ref[c] = sums[n][:, c * size : (c + 1) * size].astype(out_ref.dtype)


def own_kernel(
    blocks, own, lines, voxel_ref, line_ref, rows_ref, image_ref, tiles_ref, counts_ref,
    background_ref, activity_ref, sensitivity_ref, base_ref, measured_ref, ratio_ref, matrix_ref,
    gain_ref, slot_ref, order_ref,
):
    size = tiles_ref.shape[-1]
    width = (lines - own) // 2
    index_tiles(voxel_ref, line_ref, slot_ref, blocks, lines)
    for j in range(width):
        order_ref[j] = rows_ref[j]
    at = jnp.int32(width)
    for o in range(own):
        oblique = functools.reduce(jnp.logical_or, [rows_ref[j] == o for j in range(width)])
        order_ref[jnp.where(oblique, own, at)] = o
        at = at + jnp.where(oblique, 0, 1)
    image = image_ref[...]
    for start in range(0, own, width):
        which = [order_ref[start + c] for c in range(width)]
        sums = project(image, tiles_ref, slot_ref, range(blocks), which, lines)
        for c, row in enumerate(which):
            base = sums[:, c * size : (c + 1) * size].T + background_ref[row].astype(jnp.float32)
            measured = counts_ref[row].astype(jnp.float32)
            if start == 0:
                base_ref[c] = base
                measured_ref[c] = measured
            else:
                ratio_ref[start - width + c] = (measured / base).astype(ratio_ref.dtype)
    away = (1 - home_half()) * (blocks // 2)
    for v in range(blocks):
        voxel = lax.rem(away + v, blocks)
        for c in range(lines):
            line = order_ref[c] if c < own else c
            matrix_ref[v * size : (v + 1) * size, c * size : (c + 1) * size] = tile_of(
                tiles_ref, slot_ref, voxel, line, lines
            )
    fill_gain(size, activity_ref, sensitivity_ref, gain_ref)


def oblique_kernel(slabs, forth_ref, back_ref, base_ref, measured_ref, out_ref):
    _, has_forth, has_back = place(slabs)
    for j in range(out_ref.shape[0]):
        forth = forth_ref[j].astype(jnp.float32)
        back = back_ref[j].astype(jnp.float32)
        extra = jnp.where(has_forth, forth, 0.0) + jnp.where(has_back, back, 0.0)
        out_ref[j] = (measured_ref[j] / (base_ref[j] + extra.T)).astype(out_ref.dtype)


def own_back_kernel(own, matrix_ref, oblique_ref, ratio_ref, out_ref):
    size = ratio_ref.shape[1]
    ratios = jnp.concatenate([oblique_ref[...], ratio_ref[...]], axis=0)
    ratios = ratios.reshape(own * size, -1)
    out_ref[...] = jnp.dot(
        matrix_ref[:, : own * size], ratios, preferred_element_type=jnp.float32
    )


def fill_gain(size, activity_ref, sensitivity_ref, gain_ref):
    count = gain_ref.shape[0] // size
    first = home_half() * count
    for n in range(count):
        at = pl.multiple_of((first + n) * size, size)
        values = activity_ref[pl.ds(at, size)].astype(jnp.float32)
        sens = sensitivity_ref[pl.ds(first + n, 1)]
        gain = values / jnp.broadcast_to(sens, (size, size)).T
        gain_ref[n * size : (n + 1) * size] = gain * (1.0 / CHIP_SCALE)


def edge_back_kernel(slabs, own, start, matrix_ref, back_ref, forth_ref, own_ref, out_ref):
    size = forth_ref.shape[1]
    rows = out_ref.shape[0]
    odd, has_forth, has_back = place(slabs)
    forth = jnp.where(has_forth, forth_ref[...], jnp.zeros_like(forth_ref))
    back = jnp.where(has_back, back_ref[...], jnp.zeros_like(back_ref))
    left = jnp.where(odd == 0, back, forth)
    right = jnp.where(odd == 0, forth, back)
    ratios = jnp.concatenate([left, right], axis=0)
    ratios = ratios.reshape(ratios.shape[0] * size, -1)
    sums = jnp.dot(
        matrix_ref[start : start + rows, own * size :], ratios, preferred_element_type=jnp.float32
    )
    out_ref[...] = sums + own_ref[start : start + rows]


def write_rows_kernel(half_rows, places, *refs):
    out_hbm, sem = refs[-2:]
    odd = home_half()
    copies = []
    for n, (turn, start) in enumerate(places):
        count = refs[n].shape[0]
        at = pl.multiple_of((odd + turn) % 2 * half_rows + start, 16)
        copies.append(
            pltpu.make_async_copy(refs[n], out_hbm.at[pl.ds(at, count)], sem.at[n])
        )
    for copy in copies:
        copy.start()
    for copy in copies:
        copy.wait()


def body(
    slabs, angles, activity, sensitivity, system_tiles, tile_voxel, tile_line, oblique_rows,
    counts, background,
):
    size = system_tiles.shape[-1]
    frames = activity.shape[1]
    blocks = activity.shape[0] // size
    own = counts.shape[2] // size
    width = oblique_rows.shape[-1]
    lines = own + 2 * width
    half = blocks // 2
    tiles = system_tiles[0, 0]
    voxel = tile_voxel[0, 0]
    line = tile_line[0, 0]
    rows = oblique_rows[0, 0]
    measured = counts[0, 0].reshape(own, size, frames)
    additive = background[0, 0].reshape(own, size, frames)

    forth = []
    for s in range(slabs):
        for a in range(angles):
            t = s - 1 if a % 2 == 0 else s + 1
            here = s * angles + a
            there = t * angles + a if 0 <= t < slabs else s * angles + (a ^ 1)
            forth.append((here, there))
    back = [(there, here) for here, there in forth]
    both = ("slab", "angle")
    slots = pltpu.SMEM((blocks * (lines + 1),), jnp.int32)

    def array(dtype, *shape):
        return jax.ShapeDtypeStruct(shape, dtype)

    edge_forth, edge_back, image, held = pl.pallas_call(
        functools.partial(edge_kernel, blocks, own, lines),
        out_shape=(
            array(jnp.bfloat16, width, frames, size),
            array(jnp.bfloat16, width, frames, size),
            array(jnp.bfloat16, frames, blocks * size),
            array(jnp.bfloat16, *tiles.shape),
        ),
        in_specs=[HBM] * 4,
        out_specs=(VMEM,) * 4,
        scratch_shapes=[
            pltpu.SMEM(voxel.shape, jnp.int32),
            pltpu.SMEM(line.shape, jnp.int32),
            pltpu.VMEM(activity.shape, activity.dtype),
            slots,
            pltpu.SemaphoreType.DMA((3,)),
            pltpu.SemaphoreType.DMA((pl.cdiv(tiles.shape[0], PIECE),)),
        ],
        compiler_params=params(),
        name="edge_partials",
    )(*[pltpu.with_memory_space_constraint(a, pltpu.HBM) for a in (voxel, line, activity, tiles)])
    got_forth = lax.ppermute(edge_forth, both, forth)
    got_back = lax.ppermute(edge_back, both, back)
    half_rows = half * size
    base, taken, ratio, matrix, gain = pl.pallas_call(
        functools.partial(own_kernel, blocks, own, lines),
        out_shape=(
            array(jnp.float32, width, size, frames),
            array(jnp.float32, width, size, frames),
            array(jnp.bfloat16, own - width, size, frames),
            array(jnp.bfloat16, blocks * size, lines * size),
            array(jnp.float32, half_rows, frames),
        ),
        in_specs=[SMEM] * 3 + [VMEM] * 6,
        out_specs=(VMEM,) * 5,
        scratch_shapes=[slots, pltpu.SMEM((own + 1,), jnp.int32)],
        compiler_params=params(),
        name="own_partials",
    )(
        voxel, line, rows, image, held, measured, additive, activity,
        sensitivity.reshape(blocks, size),
    )
    oblique = pl.pallas_call(
        functools.partial(oblique_kernel, slabs),
        out_shape=array(jnp.bfloat16, width, size, frames),
        in_specs=[VMEM] * 4,
        out_specs=VMEM,
        compiler_params=params(),
        name="oblique_ratios",
    )(got_forth, got_back, base, taken)
    beside_forth = lax.ppermute(oblique, both, forth)
    beside_back = lax.ppermute(oblique, both, back)
    own_back = pl.pallas_call(
        functools.partial(own_back_kernel, own),
        out_shape=array(jnp.float32, blocks * size, frames),
        in_specs=[VMEM] * 3,
        out_specs=VMEM,
        compiler_params=params(),
        name="own_back",
    )(matrix, oblique, ratio)

    def edge_rows(start, count, name):
        return pl.pallas_call(
            functools.partial(edge_back_kernel, slabs, own, start),
            out_shape=array(jnp.float32, count, frames),
            in_specs=[VMEM] * 4,
            out_specs=VMEM,
            compiler_params=params(),
            name=name,
        )(matrix, beside_back, beside_forth, own_back)

    def wide(values):
        return values.astype(jnp.float32)

    def write_rows(image_now, name, *parts):
        values = [part[0] for part in parts]
        places = [part[1:] for part in parts]
        before = [] if image_now is None else [image_now]
        return pl.pallas_call(
            functools.partial(write_rows_kernel, half_rows, places),
            out_shape=array(jnp.bfloat16, blocks * size, frames),
            in_specs=[VMEM] * len(values) + [HBM] * len(before),
            out_specs=HBM,
            scratch_shapes=[pltpu.SemaphoreType.DMA((len(values),))],
            input_output_aliases={len(values): 0} if before else {},
            compiler_params=params(),
            name=name,
        )(*values, *before)

    pairs = [(a, a ^ 1) for a in range(angles)]
    cuts = [0, FIRST_PART * half_rows // 16, half_rows]
    spans = [slice(at, end) for at, end in zip(cuts[:-1], cuts[1:])]
    first, later = spans
    away = edge_rows(0, first.stop, "edge_back_first")
    got = [lax.ppermute((away * PART_SCALE).astype(jnp.float16), "angle", pairs)]
    rest = edge_rows(first.stop, 2 * half_rows - first.stop, "edge_back_rest")
    away = rest[: later.stop - later.start] * PART_SCALE
    got.append(lax.ppermute(away.astype(jnp.float16), "angle", pairs))
    home = rest[later.stop - later.start :]
    written = []
    for n, (at, end) in enumerate(zip(cuts[:-1], cuts[1:])):
        span = spans[n]
        chip = (home[span] + wide(got[n]) * (1.0 / PART_SCALE)) * CHIP_SCALE
        if angles == 4:
            chip = lax.optimization_barrier(chip.astype(jnp.float16))
            across = lax.ppermute(chip, "angle", [(a, a ^ 3) for a in range(angles)])
            if written:
                across, rows_away = lax.optimization_barrier((across, rows_away))
                written[-1] = (rows_away,) + written[-1][1:]
            total = wide(chip) + wide(across)
        else:
            groups = [[a for a in range(angles) if (a + a // 2) % 2 == n] for n in range(2)]
            total = lax.psum(chip, "angle", axis_index_groups=groups)
        rows_home = (gain[span] * total).astype(jnp.bfloat16)
        rows_home = lax.optimization_barrier(rows_home)
        rows_away = lax.ppermute(rows_home, "angle", pairs)
        written += [(rows_home, 0, at), (rows_away, 1, at)]
    updated = write_rows(None, "write_first", *written[:-1])
    return write_rows(updated, "write_last", written[-1])


def solution(mesh):
    placed = (
        P(("groups", "slab"), None),
        P(("groups", "slab")),
        P(("groups", "slab"), "angle", None, None, None),
        P(("groups", "slab"), "angle", None),
        P(("groups", "slab"), "angle", None),
        P(("groups", "slab"), "angle", None),
        P(("groups", "slab"), "angle", None, None),
        P(("groups", "slab"), "angle", None, None),
    )
    return jax.shard_map(
        functools.partial(body, mesh.shape["slab"], mesh.shape["angle"]),
        mesh=mesh,
        in_specs=placed,
        out_specs=P(("groups", "slab"), None),
        check_vma=False,
    )
```

```python
import functools

import jax
import jax.numpy as jnp
from jax import lax
from jax.experimental import pallas as pl
from jax.experimental.pallas import tpu as pltpu
from jax.sharding import PartitionSpec as P

VMEM = pl.BlockSpec(memory_space=pltpu.VMEM)
SMEM = pl.BlockSpec(memory_space=pltpu.SMEM)
HBM = pl.BlockSpec(memory_space=pltpu.HBM)
PART_SCALE = 256.0
CHIP_SCALE = 128.0
GROUP = 3
PIECE = 24
FIRST_PART = 7


def params(mebibytes=16):
    return pltpu.CompilerParams(vmem_limit_bytes=mebibytes * 1024 * 1024)


def place(slabs):
    slab = lax.axis_index("slab")
    odd = lax.axis_index("angle") % 2
    left = slab > 0
    right = slab < slabs - 1
    even = odd == 0
    forth = jnp.logical_or(jnp.logical_and(even, right), jnp.logical_and(~even, left))
    back = jnp.logical_or(jnp.logical_and(even, left), jnp.logical_and(~even, right))
    return odd, forth, back


def home_half():
    angle = lax.axis_index("angle")
    return (angle + angle // 2) % 2


def index_tiles(voxel_ref, line_ref, slot_ref, blocks, lines):
    stride = lines + 1
    for n in range(blocks * stride):
        slot_ref[n] = -1
    for k in range(voxel_ref.shape[-1]):
        slot_ref[voxel_ref[k] * stride + line_ref[k]] = k


def tile_of(tiles_ref, slot_ref, voxel, line, lines):
    slot = slot_ref[voxel * (lines + 1) + line]
    tile = tiles_ref[jnp.maximum(slot, 0)]
    return jnp.where(slot >= 0, tile, jnp.zeros_like(tile))


def project(image, tiles_ref, slot_ref, voxels, which, lines):
    weights = jnp.concatenate(
        [
            jnp.concatenate([tile_of(tiles_ref, slot_ref, v, c, lines) for c in which], axis=1)
            for v in voxels
        ],
        axis=0,
    )
    return jnp.dot(image, weights, preferred_element_type=jnp.float32)


def edge_kernel(
    blocks, own, lines, voxel_hbm, line_hbm, activity_hbm, tiles_hbm,
    forth_ref, back_ref, image_ref, tiles_ref,
    voxel_ref, line_ref, activity_ref, slot_ref, small_sem, tile_sem,
):
    size = tiles_ref.shape[-1]
    total = tiles_ref.shape[0]
    width = (lines - own) // 2
    first = [
        pltpu.make_async_copy(voxel_hbm, voxel_ref, small_sem.at[0]),
        pltpu.make_async_copy(line_hbm, line_ref, small_sem.at[1]),
        pltpu.make_async_copy(activity_hbm, activity_ref, small_sem.at[2]),
    ]
    pieces = []
    for n, start in enumerate(range(0, total, PIECE)):
        span = pl.ds(start, min(PIECE, total - start))
        pieces.append(
            pltpu.make_async_copy(tiles_hbm.at[span], tiles_ref.at[span], tile_sem.at[n])
        )
    for copy in first:
        copy.start()
    for copy in pieces:
        copy.start(priority=1)
    first[0].wait()
    first[1].wait()
    index_tiles(voxel_ref, line_ref, slot_ref, blocks, lines)
    first[2].wait()
    for v in range(blocks):
        image_ref[:, v * size : (v + 1) * size] = activity_ref[v * size : (v + 1) * size, :].T
    odd = lax.axis_index("angle") % 2
    outs = (
        (forth_ref, own + width * odd),
        (back_ref, own + width * (1 - odd)),
    )
    sums = [None, None]
    waited = 0
    for low in range(0, blocks, GROUP):
        high = min(low + GROUP, blocks)
        needed = len(pieces) if high == blocks else min(len(pieces), pl.cdiv(high * lines, PIECE))
        for copy in pieces[waited:needed]:
            copy.wait()
        waited = needed
        image = image_ref[:, low * size : high * size]
        for n, (_, start) in enumerate(outs):
            which = [start + c for c in range(width)]
            part = project(image, tiles_ref, slot_ref, range(low, high), which, lines)
            sums[n] = part if sums[n] is None else sums[n] + part
    for n, (out_ref, _) in enumerate(outs):
        for c in range(width):
            out_ref[c] = sums[n][:, c * size : (c + 1) * size].astype(out_ref.dtype)


def own_kernel(
    blocks, own, lines, voxel_ref, line_ref, rows_ref, image_ref, tiles_ref, counts_ref,
    background_ref, activity_ref, sensitivity_ref, base_ref, measured_ref, ratio_ref, matrix_ref,
    gain_ref, slot_ref, order_ref,
):
    size = tiles_ref.shape[-1]
    width = (lines - own) // 2
    index_tiles(voxel_ref, line_ref, slot_ref, blocks, lines)
    for j in range(width):
        order_ref[j] = rows_ref[j]
    at = jnp.int32(width)
    for o in range(own):
        oblique = functools.reduce(jnp.logical_or, [rows_ref[j] == o for j in range(width)])
        order_ref[jnp.where(oblique, own, at)] = o
        at = at + jnp.where(oblique, 0, 1)
    image = image_ref[...]
    for start in range(0, own, width):
        which = [order_ref[start + c] for c in range(width)]
        sums = project(image, tiles_ref, slot_ref, range(blocks), which, lines)
        for c, row in enumerate(which):
            base = sums[:, c * size : (c + 1) * size].T + background_ref[row].astype(jnp.float32)
            measured = counts_ref[row].astype(jnp.float32)
            if start == 0:
                base_ref[c] = base
                measured_ref[c] = measured
            else:
                ratio_ref[start - width + c] = (measured / base).astype(ratio_ref.dtype)
    away = (1 - home_half()) * (blocks // 2)
    for v in range(blocks):
        voxel = lax.rem(away + v, blocks)
        for c in range(lines):
            line = order_ref[c] if c < own else c
            matrix_ref[v * size : (v + 1) * size, c * size : (c + 1) * size] = tile_of(
                tiles_ref, slot_ref, voxel, line, lines
            )
    fill_gain(size, activity_ref, sensitivity_ref, gain_ref)


def oblique_kernel(slabs, forth_ref, back_ref, base_ref, measured_ref, out_ref):
    _, has_forth, has_back = place(slabs)
    for j in range(out_ref.shape[0]):
        forth = forth_ref[j].astype(jnp.float32)
        back = back_ref[j].astype(jnp.float32)
        extra = jnp.where(has_forth, forth, 0.0) + jnp.where(has_back, back, 0.0)
        out_ref[j] = (measured_ref[j] / (base_ref[j] + extra.T)).astype(out_ref.dtype)


def own_back_kernel(own, matrix_ref, oblique_ref, ratio_ref, out_ref):
    size = ratio_ref.shape[1]
    ratios = jnp.concatenate([oblique_ref[...], ratio_ref[...]], axis=0)
    ratios = ratios.reshape(own * size, -1)
    out_ref[...] = jnp.dot(
        matrix_ref[:, : own * size], ratios, preferred_element_type=jnp.float32
    )


def fill_gain(size, activity_ref, sensitivity_ref, gain_ref):
    count = gain_ref.shape[0] // size
    first = home_half() * count
    for n in range(count):
        at = pl.multiple_of((first + n) * size, size)
        values = activity_ref[pl.ds(at, size)].astype(jnp.float32)
        sens = sensitivity_ref[pl.ds(first + n, 1)]
        gain = values / jnp.broadcast_to(sens, (size, size)).T
        gain_ref[n * size : (n + 1) * size] = gain * (1.0 / CHIP_SCALE)


def edge_back_kernel(slabs, own, start, matrix_ref, back_ref, forth_ref, own_ref, out_ref):
    size = forth_ref.shape[1]
    rows = out_ref.shape[0]
    odd, has_forth, has_back = place(slabs)
    forth = jnp.where(has_forth, forth_ref[...], jnp.zeros_like(forth_ref))
    back = jnp.where(has_back, back_ref[...], jnp.zeros_like(back_ref))
    left = jnp.where(odd == 0, back, forth)
    right = jnp.where(odd == 0, forth, back)
    ratios = jnp.concatenate([left, right], axis=0)
    ratios = ratios.reshape(ratios.shape[0] * size, -1)
    sums = jnp.dot(
        matrix_ref[start : start + rows, own * size :], ratios, preferred_element_type=jnp.float32
    )
    out_ref[...] = sums + own_ref[start : start + rows]


def write_rows_kernel(half_rows, places, *refs):
    out_hbm, sem = refs[-2:]
    odd = home_half()
    copies = []
    for n, (turn, start) in enumerate(places):
        count = refs[n].shape[0]
        at = pl.multiple_of((odd + turn) % 2 * half_rows + start, 16)
        copies.append(
            pltpu.make_async_copy(refs[n], out_hbm.at[pl.ds(at, count)], sem.at[n])
        )
    for copy in copies:
        copy.start()
    for copy in copies:
        copy.wait()


def body(
    slabs, angles, activity, sensitivity, system_tiles, tile_voxel, tile_line, oblique_rows,
    counts, background,
):
    size = system_tiles.shape[-1]
    frames = activity.shape[1]
    blocks = activity.shape[0] // size
    own = counts.shape[2] // size
    width = oblique_rows.shape[-1]
    lines = own + 2 * width
    half = blocks // 2
    tiles = system_tiles[0, 0]
    voxel = tile_voxel[0, 0]
    line = tile_line[0, 0]
    rows = oblique_rows[0, 0]
    measured = counts[0, 0].reshape(own, size, frames)
    additive = background[0, 0].reshape(own, size, frames)

    forth = []
    for s in range(slabs):
        for a in range(angles):
            t = s - 1 if a % 2 == 0 else s + 1
            here = s * angles + a
            there = t * angles + a if 0 <= t < slabs else s * angles + (a ^ 1)
            forth.append((here, there))
    back = [(there, here) for here, there in forth]
    both = ("slab", "angle")
    slots = pltpu.SMEM((blocks * (lines + 1),), jnp.int32)

    def array(dtype, *shape):
        return jax.ShapeDtypeStruct(shape, dtype)

    edge_forth, edge_back, image, held = pl.pallas_call(
        functools.partial(edge_kernel, blocks, own, lines),
        out_shape=(
            array(jnp.bfloat16, width, frames, size),
            array(jnp.bfloat16, width, frames, size),
            array(jnp.bfloat16, frames, blocks * size),
            array(jnp.bfloat16, *tiles.shape),
        ),
        in_specs=[HBM] * 4,
        out_specs=(VMEM,) * 4,
        scratch_shapes=[
            pltpu.SMEM(voxel.shape, jnp.int32),
            pltpu.SMEM(line.shape, jnp.int32),
            pltpu.VMEM(activity.shape, activity.dtype),
            slots,
            pltpu.SemaphoreType.DMA((3,)),
            pltpu.SemaphoreType.DMA((pl.cdiv(tiles.shape[0], PIECE),)),
        ],
        compiler_params=params(),
        name="edge_partials",
    )(*[pltpu.with_memory_space_constraint(a, pltpu.HBM) for a in (voxel, line, activity, tiles)])
    got_forth = lax.ppermute(edge_forth, both, forth)
    got_back = lax.ppermute(edge_back, both, back)
    half_rows = half * size
    base, taken, ratio, matrix, gain = pl.pallas_call(
        functools.partial(own_kernel, blocks, own, lines),
        out_shape=(
            array(jnp.float32, width, size, frames),
            array(jnp.float32, width, size, frames),
            array(jnp.bfloat16, own - width, size, frames),
            array(jnp.bfloat16, blocks * size, lines * size),
            array(jnp.float32, half_rows, frames),
        ),
        in_specs=[SMEM] * 3 + [VMEM] * 6,
        out_specs=(VMEM,) * 5,
        scratch_shapes=[slots, pltpu.SMEM((own + 1,), jnp.int32)],
        compiler_params=params(),
        name="own_partials",
    )(
        voxel, line, rows, image, held, measured, additive, activity,
        sensitivity.reshape(blocks, size),
    )
    oblique = pl.pallas_call(
        functools.partial(oblique_kernel, slabs),
        out_shape=array(jnp.bfloat16, width, size, frames),
        in_specs=[VMEM] * 4,
        out_specs=VMEM,
        compiler_params=params(),
        name="oblique_ratios",
    )(got_forth, got_back, base, taken)
    beside_forth = lax.ppermute(oblique, both, forth)
    beside_back = lax.ppermute(oblique, both, back)
    own_back = pl.pallas_call(
        functools.partial(own_back_kernel, own),
        out_shape=array(jnp.float32, blocks * size, frames),
        in_specs=[VMEM] * 3,
        out_specs=VMEM,
        compiler_params=params(),
        name="own_back",
    )(matrix, oblique, ratio)

    def edge_rows(start, count, name):
        return pl.pallas_call(
            functools.partial(edge_back_kernel, slabs, own, start),
            out_shape=array(jnp.float32, count, frames),
            in_specs=[VMEM] * 4,
            out_specs=VMEM,
            compiler_params=params(),
            name=name,
        )(matrix, beside_back, beside_forth, own_back)

    def wide(values):
        return values.astype(jnp.float32)

    def write_rows(image_now, name, *parts):
        values = [part[0] for part in parts]
        places = [part[1:] for part in parts]
        before = [] if image_now is None else [image_now]
        return pl.pallas_call(
            functools.partial(write_rows_kernel, half_rows, places),
            out_shape=array(jnp.bfloat16, blocks * size, frames),
            in_specs=[VMEM] * len(values) + [HBM] * len(before),
            out_specs=HBM,
            scratch_shapes=[pltpu.SemaphoreType.DMA((len(values),))],
            input_output_aliases={len(values): 0} if before else {},
            compiler_params=params(),
            name=name,
        )(*values, *before)

    pairs = [(a, a ^ 1) for a in range(angles)]
    cuts = [0, FIRST_PART * half_rows // 16, half_rows]
    spans = [slice(at, end) for at, end in zip(cuts[:-1], cuts[1:])]
    first, later = spans
    away = edge_rows(0, first.stop, "edge_back_first")
    got = [lax.ppermute((away * PART_SCALE).astype(jnp.float16), "angle", pairs)]
    rest = edge_rows(first.stop, 2 * half_rows - first.stop, "edge_back_rest")
    away = rest[: later.stop - later.start] * PART_SCALE
    got.append(lax.ppermute(away.astype(jnp.float16), "angle", pairs))
    home = rest[later.stop - later.start :]
    written = []
    for n, (at, end) in enumerate(zip(cuts[:-1], cuts[1:])):
        span = spans[n]
        chip = (home[span] + wide(got[n]) * (1.0 / PART_SCALE)) * CHIP_SCALE
        if angles == 4:
            chip = lax.optimization_barrier(chip.astype(jnp.float16))
            across = lax.ppermute(chip, "angle", [(a, a ^ 3) for a in range(angles)])
            if written:
                across, rows_away = lax.optimization_barrier((across, rows_away))
                written[-1] = (rows_away,) + written[-1][1:]
            total = wide(chip) + wide(across)
        else:
            groups = [[a for a in range(angles) if (a + a // 2) % 2 == n] for n in range(2)]
            total = lax.psum(chip, "angle", axis_index_groups=groups)
        rows_home = (gain[span] * total).astype(jnp.bfloat16)
        rows_home = lax.optimization_barrier(rows_home)
        rows_away = lax.ppermute(rows_home, "angle", pairs)
        written += [(rows_home, 0, at), (rows_away, 1, at)]
    updated = write_rows(None, "write_first", *written[:-1])
    return write_rows(updated, "write_last", written[-1])


def solution(mesh):
    placed = (
        P(("groups", "slab"), None),
        P(("groups", "slab")),
        P(("groups", "slab"), "angle", None, None, None),
        P(("groups", "slab"), "angle", None),
        P(("groups", "slab"), "angle", None),
        P(("groups", "slab"), "angle", None),
        P(("groups", "slab"), "angle", None, None),
        P(("groups", "slab"), "angle", None, None),
    )
    return jax.shard_map(
        functools.partial(body, mesh.shape["slab"], mesh.shape["angle"]),
        mesh=mesh,
        in_specs=placed,
        out_specs=P(("groups", "slab"), None),
        check_vma=False,
    )
```

```python
import functools

import jax
import jax.numpy as jnp
from jax import lax
from jax.experimental import pallas as pl
from jax.experimental.pallas import tpu as pltpu
from jax.sharding import PartitionSpec as P

VMEM = pl.BlockSpec(memory_space=pltpu.VMEM)
SMEM = pl.BlockSpec(memory_space=pltpu.SMEM)
HBM = pl.BlockSpec(memory_space=pltpu.HBM)
PART_SCALE = 256.0
CHIP_SCALE = 128.0
GROUP = 3
PIECE = 24
FIRST_PART = 7


def params(mebibytes=16):
    return pltpu.CompilerParams(vmem_limit_bytes=mebibytes * 1024 * 1024)


def place(slabs):
    slab = lax.axis_index("slab")
    odd = lax.axis_index("angle") % 2
    left = slab > 0
    right = slab < slabs - 1
    even = odd == 0
    forth = jnp.logical_or(jnp.logical_and(even, right), jnp.logical_and(~even, left))
    back = jnp.logical_or(jnp.logical_and(even, left), jnp.logical_and(~even, right))
    return odd, forth, back


def home_half():
    angle = lax.axis_index("angle")
    return (angle + angle // 2) % 2


def index_tiles(voxel_ref, line_ref, slot_ref, blocks, lines):
    stride = lines + 1
    for n in range(blocks * stride):
        slot_ref[n] = -1
    for k in range(voxel_ref.shape[-1]):
        slot_ref[voxel_ref[k] * stride + line_ref[k]] = k


def tile_of(tiles_ref, slot_ref, voxel, line, lines):
    slot = slot_ref[voxel * (lines + 1) + line]
    tile = tiles_ref[jnp.maximum(slot, 0)]
    return jnp.where(slot >= 0, tile, jnp.zeros_like(tile))


def project(image, tiles_ref, slot_ref, voxels, which, lines):
    weights = jnp.concatenate(
        [
            jnp.concatenate([tile_of(tiles_ref, slot_ref, v, c, lines) for c in which], axis=1)
            for v in voxels
        ],
        axis=0,
    )
    return jnp.dot(image, weights, preferred_element_type=jnp.float32)


def edge_kernel(
    blocks, own, lines, voxel_hbm, line_hbm, activity_hbm, tiles_hbm,
    forth_ref, back_ref, image_ref, tiles_ref,
    voxel_ref, line_ref, activity_ref, slot_ref, small_sem, tile_sem,
):
    size = tiles_ref.shape[-1]
    total = tiles_ref.shape[0]
    width = (lines - own) // 2
    first = [
        pltpu.make_async_copy(voxel_hbm, voxel_ref, small_sem.at[0]),
        pltpu.make_async_copy(line_hbm, line_ref, small_sem.at[1]),
        pltpu.make_async_copy(activity_hbm, activity_ref, small_sem.at[2]),
    ]
    pieces = []
    for n, start in enumerate(range(0, total, PIECE)):
        span = pl.ds(start, min(PIECE, total - start))
        pieces.append(
            pltpu.make_async_copy(tiles_hbm.at[span], tiles_ref.at[span], tile_sem.at[n])
        )
    for copy in first:
        copy.start()
    for copy in pieces:
        copy.start(priority=1)
    first[0].wait()
    first[1].wait()
    index_tiles(voxel_ref, line_ref, slot_ref, blocks, lines)
    first[2].wait()
    for v in range(blocks):
        image_ref[:, v * size : (v + 1) * size] = activity_ref[v * size : (v + 1) * size, :].T
    odd = lax.axis_index("angle") % 2
    which = [own + width * odd + c for c in range(width)]
    which += [own + width * (1 - odd) + c for c in range(width)]
    sums = None
    waited = 0
    for low in range(0, blocks, GROUP):
        high = min(low + GROUP, blocks)
        needed = len(pieces) if high == blocks else min(len(pieces), pl.cdiv(high * lines, PIECE))
        for copy in pieces[waited:needed]:
            copy.wait()
        waited = needed
        image = image_ref[:, low * size : high * size]
        part = project(image, tiles_ref, slot_ref, range(low, high), which, lines)
        sums = part if sums is None else sums + part
    for c in range(width):
        forth_ref[c] = sums[:, c * size : (c + 1) * size].astype(forth_ref.dtype)
        back_ref[c] = sums[:, (width + c) * size : (width + c + 1) * size].astype(back_ref.dtype)


def own_kernel(
    blocks, own, lines, voxel_ref, line_ref, rows_ref, image_ref, tiles_ref, counts_ref,
    background_ref, activity_ref, sensitivity_ref, base_ref, measured_ref, ratio_ref, matrix_ref,
    gain_ref, slot_ref, order_ref,
):
    size = tiles_ref.shape[-1]
    width = (lines - own) // 2
    index_tiles(voxel_ref, line_ref, slot_ref, blocks, lines)
    for j in range(width):
        order_ref[j] = rows_ref[j]
    at = jnp.int32(width)
    for o in range(own):
        oblique = functools.reduce(jnp.logical_or, [rows_ref[j] == o for j in range(width)])
        order_ref[jnp.where(oblique, own, at)] = o
        at = at + jnp.where(oblique, 0, 1)
    image = image_ref[...]
    for start in range(0, own, width):
        which = [order_ref[start + c] for c in range(width)]
        sums = project(image, tiles_ref, slot_ref, range(blocks), which, lines)
        for c, row in enumerate(which):
            base = sums[:, c * size : (c + 1) * size].T + background_ref[row].astype(jnp.float32)
            measured = counts_ref[row].astype(jnp.float32)
            if start == 0:
                base_ref[c] = base
                measured_ref[c] = measured
            else:
                ratio_ref[start - width + c] = (measured / base).astype(ratio_ref.dtype)
    away = (1 - home_half()) * (blocks // 2)
    for v in range(blocks):
        voxel = lax.rem(away + v, blocks)
        for c in range(lines):
            line = order_ref[c] if c < own else c
            matrix_ref[v * size : (v + 1) * size, c * size : (c + 1) * size] = tile_of(
                tiles_ref, slot_ref, voxel, line, lines
            )
    fill_gain(size, activity_ref, sensitivity_ref, gain_ref)


def oblique_kernel(slabs, forth_ref, back_ref, base_ref, measured_ref, out_ref):
    _, has_forth, has_back = place(slabs)
    for j in range(out_ref.shape[0]):
        forth = forth_ref[j].astype(jnp.float32)
        back = back_ref[j].astype(jnp.float32)
        extra = jnp.where(has_forth, forth, 0.0) + jnp.where(has_back, back, 0.0)
        out_ref[j] = (measured_ref[j] / (base_ref[j] + extra.T)).astype(out_ref.dtype)


def own_back_kernel(own, matrix_ref, oblique_ref, ratio_ref, out_ref):
    size = ratio_ref.shape[1]
    ratios = jnp.concatenate([oblique_ref[...], ratio_ref[...]], axis=0)
    ratios = ratios.reshape(own * size, -1)
    out_ref[...] = jnp.dot(
        matrix_ref[:, : own * size], ratios, preferred_element_type=jnp.float32
    )


def fill_gain(size, activity_ref, sensitivity_ref, gain_ref):
    count = gain_ref.shape[0] // size
    first = home_half() * count
    for n in range(count):
        at = pl.multiple_of((first + n) * size, size)
        values = activity_ref[pl.ds(at, size)].astype(jnp.float32)
        sens = sensitivity_ref[pl.ds(first + n, 1)]
        gain = values / jnp.broadcast_to(sens, (size, size)).T
        gain_ref[n * size : (n + 1) * size] = gain * (1.0 / CHIP_SCALE)


def edge_back_kernel(slabs, own, start, matrix_ref, back_ref, forth_ref, own_ref, out_ref):
    size = forth_ref.shape[1]
    rows = out_ref.shape[0]
    odd, has_forth, has_back = place(slabs)
    forth = jnp.where(has_forth, forth_ref[...], jnp.zeros_like(forth_ref))
    back = jnp.where(has_back, back_ref[...], jnp.zeros_like(back_ref))
    left = jnp.where(odd == 0, back, forth)
    right = jnp.where(odd == 0, forth, back)
    ratios = jnp.concatenate([left, right], axis=0)
    ratios = ratios.reshape(ratios.shape[0] * size, -1)
    sums = jnp.dot(
        matrix_ref[start : start + rows, own * size :], ratios, preferred_element_type=jnp.float32
    )
    out_ref[...] = sums + own_ref[start : start + rows]


def write_rows_kernel(half_rows, places, *refs):
    out_hbm, sem = refs[-2:]
    odd = home_half()
    copies = []
    for n, (turn, start) in enumerate(places):
        count = refs[n].shape[0]
        at = pl.multiple_of((odd + turn) % 2 * half_rows + start, 16)
        copies.append(
            pltpu.make_async_copy(refs[n], out_hbm.at[pl.ds(at, count)], sem.at[n])
        )
    for copy in copies:
        copy.start()
    for copy in copies:
        copy.wait()


def body(
    slabs, angles, activity, sensitivity, system_tiles, tile_voxel, tile_line, oblique_rows,
    counts, background,
):
    size = system_tiles.shape[-1]
    frames = activity.shape[1]
    blocks = activity.shape[0] // size
    own = counts.shape[2] // size
    width = oblique_rows.shape[-1]
    lines = own + 2 * width
    half = blocks // 2
    tiles = system_tiles[0, 0]
    voxel = tile_voxel[0, 0]
    line = tile_line[0, 0]
    rows = oblique_rows[0, 0]
    measured = counts[0, 0].reshape(own, size, frames)
    additive = background[0, 0].reshape(own, size, frames)

    forth = []
    for s in range(slabs):
        for a in range(angles):
            t = s - 1 if a % 2 == 0 else s + 1
            here = s * angles + a
            there = t * angles + a if 0 <= t < slabs else s * angles + (a ^ 1)
            forth.append((here, there))
    back = [(there, here) for here, there in forth]
    both = ("slab", "angle")
    slots = pltpu.SMEM((blocks * (lines + 1),), jnp.int32)

    def array(dtype, *shape):
        return jax.ShapeDtypeStruct(shape, dtype)

    edge_forth, edge_back, image, held = pl.pallas_call(
        functools.partial(edge_kernel, blocks, own, lines),
        out_shape=(
            array(jnp.bfloat16, width, frames, size),
            array(jnp.bfloat16, width, frames, size),
            array(jnp.bfloat16, frames, blocks * size),
            array(jnp.bfloat16, *tiles.shape),
        ),
        in_specs=[HBM] * 4,
        out_specs=(VMEM,) * 4,
        scratch_shapes=[
            pltpu.SMEM(voxel.shape, jnp.int32),
            pltpu.SMEM(line.shape, jnp.int32),
            pltpu.VMEM(activity.shape, activity.dtype),
            slots,
            pltpu.SemaphoreType.DMA((3,)),
            pltpu.SemaphoreType.DMA((pl.cdiv(tiles.shape[0], PIECE),)),
        ],
        compiler_params=params(),
        name="edge_partials",
    )(*[pltpu.with_memory_space_constraint(a, pltpu.HBM) for a in (voxel, line, activity, tiles)])
    got_forth = lax.ppermute(edge_forth, both, forth)
    got_back = lax.ppermute(edge_back, both, back)
    half_rows = half * size
    base, taken, ratio, matrix, gain = pl.pallas_call(
        functools.partial(own_kernel, blocks, own, lines),
        out_shape=(
            array(jnp.float32, width, size, frames),
            array(jnp.float32, width, size, frames),
            array(jnp.bfloat16, own - width, size, frames),
            array(jnp.bfloat16, blocks * size, lines * size),
            array(jnp.float32, half_rows, frames),
        ),
        in_specs=[SMEM] * 3 + [VMEM] * 6,
        out_specs=(VMEM,) * 5,
        scratch_shapes=[slots, pltpu.SMEM((own + 1,), jnp.int32)],
        compiler_params=params(),
        name="own_partials",
    )(
        voxel, line, rows, image, held, measured, additive, activity,
        sensitivity.reshape(blocks, size),
    )
    oblique = pl.pallas_call(
        functools.partial(oblique_kernel, slabs),
        out_shape=array(jnp.bfloat16, width, size, frames),
        in_specs=[VMEM] * 4,
        out_specs=VMEM,
        compiler_params=params(),
        name="oblique_ratios",
    )(got_forth, got_back, base, taken)
    beside_forth = lax.ppermute(oblique, both, forth)
    beside_back = lax.ppermute(oblique, both, back)
    own_back = pl.pallas_call(
        functools.partial(own_back_kernel, own),
        out_shape=array(jnp.float32, blocks * size, frames),
        in_specs=[VMEM] * 3,
        out_specs=VMEM,
        compiler_params=params(),
        name="own_back",
    )(matrix, oblique, ratio)

    def edge_rows(start, count, name):
        return pl.pallas_call(
            functools.partial(edge_back_kernel, slabs, own, start),
            out_shape=array(jnp.float32, count, frames),
            in_specs=[VMEM] * 4,
            out_specs=VMEM,
            compiler_params=params(),
            name=name,
        )(matrix, beside_back, beside_forth, own_back)

    def wide(values):
        return values.astype(jnp.float32)

    def write_rows(image_now, name, *parts):
        values = [part[0] for part in parts]
        places = [part[1:] for part in parts]
        before = [] if image_now is None else [image_now]
        return pl.pallas_call(
            functools.partial(write_rows_kernel, half_rows, places),
            out_shape=array(jnp.bfloat16, blocks * size, frames),
            in_specs=[VMEM] * len(values) + [HBM] * len(before),
            out_specs=HBM,
            scratch_shapes=[pltpu.SemaphoreType.DMA((len(values),))],
            input_output_aliases={len(values): 0} if before else {},
            compiler_params=params(),
            name=name,
        )(*values, *before)

    pairs = [(a, a ^ 1) for a in range(angles)]
    cuts = [0, FIRST_PART * half_rows // 16, half_rows]
    spans = [slice(at, end) for at, end in zip(cuts[:-1], cuts[1:])]
    first, later = spans
    away = edge_rows(0, first.stop, "edge_back_first")
    got = [lax.ppermute((away * PART_SCALE).astype(jnp.float16), "angle", pairs)]
    rest = edge_rows(first.stop, 2 * half_rows - first.stop, "edge_back_rest")
    away = rest[: later.stop - later.start] * PART_SCALE
    got.append(lax.ppermute(away.astype(jnp.float16), "angle", pairs))
    home = rest[later.stop - later.start :]
    written = []
    for n, (at, end) in enumerate(zip(cuts[:-1], cuts[1:])):
        span = spans[n]
        chip = (home[span] + wide(got[n]) * (1.0 / PART_SCALE)) * CHIP_SCALE
        if angles == 4:
            chip = lax.optimization_barrier(chip.astype(jnp.float16))
            across = lax.ppermute(chip, "angle", [(a, a ^ 3) for a in range(angles)])
            if written:
                across, rows_away = lax.optimization_barrier((across, rows_away))
                written[-1] = (rows_away,) + written[-1][1:]
            total = wide(chip) + wide(across)
        else:
            groups = [[a for a in range(angles) if (a + a // 2) % 2 == n] for n in range(2)]
            total = lax.psum(chip, "angle", axis_index_groups=groups)
        rows_home = (gain[span] * total).astype(jnp.bfloat16)
        rows_home = lax.optimization_barrier(rows_home)
        rows_away = lax.ppermute(rows_home, "angle", pairs)
        written += [(rows_home, 0, at), (rows_away, 1, at)]
    updated = write_rows(None, "write_first", *written[:-1])
    return write_rows(updated, "write_last", written[-1])


def solution(mesh):
    placed = (
        P(("groups", "slab"), None),
        P(("groups", "slab")),
        P(("groups", "slab"), "angle", None, None, None),
        P(("groups", "slab"), "angle", None),
        P(("groups", "slab"), "angle", None),
        P(("groups", "slab"), "angle", None),
        P(("groups", "slab"), "angle", None, None),
        P(("groups", "slab"), "angle", None, None),
    )
    return jax.shard_map(
        functools.partial(body, mesh.shape["slab"], mesh.shape["angle"]),
        mesh=mesh,
        in_specs=placed,
        out_specs=P(("groups", "slab"), None),
        check_vma=False,
    )
```
